1024 devices in a mesh: dp: 16 (over y, core), expert: 64 (over x, z).
Axes of the slice: x: 4, y: 8, z: 16, core: 2. Of those that a mesh axis runs over, the one named last changes fastest.
Arguments:
- out_grad: bfloat16 [16384, 4096], P(('dp', 'expert')), may hold values from -6 to 6
- hidden_acts: bfloat16 [16384, 8, 768], P(('dp', 'expert')), may hold values from -0.23925781 to 0.23925781
- gate_weights: float32 [16384, 8], P(('dp', 'expert')), may hold values from 0 to 1, as said below
- expert_idx: int32 [16384, 8], P(('dp', 'expert')), may hold values from 0 to 63, all different within a row; in each aligned block of 16 rows (0 to 15, 16 to 31, ...) at most 3 rows name the same one
- down_weight: bfloat16 [64, 768, 4096], P('expert'), may hold values from -0.09375 to 0.09375
Outputs:
- act_grad: bfloat16 [16384, 8, 768], P(('dp', 'expert'))
- logit_grad: float32 [16384, 8], P(('dp', 'expert'))
- down_grad: bfloat16 [64, 768, 4096], P('expert', 'dp')
The draws below stay inside these ranges and needn't reach their ends.
Inputs may be any that keep to these rules, and one draw needn't show every extreme that they name: `expert_idx`: each row names 8 different experts; among the 16 rows of one device no expert is named more than 3 times, a bound that some block reaches. `gate_weights`: each row is positive and sums to one.
All inputs are finite; a program needn't handle non-finite values.
Results may differ from the reference program's by a relative error of at most 0.022.
Values may be sent and summed in bfloat16 or wider, within the bound.
No kernel may reach another device: no remote copies, remote signals or barrier semaphores. Data moves between devices by JAX's collectives and lax.ppermute only.
A program may use at most 64 MiB of HBM per device.

```python
import math
import jax
import jax.numpy as jnp
import numpy as np
from jax import lax

D = 4096
TOP = 8
FW = 768
TOK_DEV = 16
EXPERTS = 64
MOST = 3
GROUP_TOK = 1024
TOKENS = 16384
N_DP = 16
N_EXPERT = 64


def draw_gate_weights(key, part):
    key = jax.random.fold_in(key, 5)
    logits = jnp.clip(0.4 * jax.random.normal(key, (TOKENS, TOP), jnp.float32), -0.8, 0.8)
    powers = jnp.exp(logits)
    return powers / jnp.sum(powers, axis=1, keepdims=True)


def block_scale(own_key, dims, cuts, least, high):
    level = 1.0
    for axis_at, shards_of in cuts:
        steps = jax.random.uniform(jax.random.fold_in(jax.random.fold_in(own_key, 6), axis_at), (shards_of,), jnp.float32, least / len(cuts), high / len(cuts))
        level = level * jnp.repeat(jnp.exp(steps), dims[axis_at] // shards_of).reshape((-1,) + (1,) * (len(dims) - 1 - axis_at))
    return level


def deal_out(own_key, own, number, rows, count, top, limit, skew):
    sequence = jax.random.permutation(own_key, count)
    packed, ordinary = load_shares(count, rows * top, limit, skew, True), load_shares(count, rows * top, limit, skew, False)
    places = jnp.arange(count)

    def named(tallies, rotation):
        used = int((tallies > 0).sum())
        fixed = max(1, used // 4)
        shifted = fixed + (places - fixed + rotation * (used - fixed)) % max(1, count - fixed)
        return jnp.zeros((count,), jnp.int32).at[sequence[jnp.where(places < fixed, places, shifted)]].set(jnp.asarray(tallies, jnp.int32))

    tallies = jnp.where(number % 4 == 0, named(packed, number // 4), named(ordinary, number - number // 4 - 1))
    mixed = jax.random.permutation(jax.random.fold_in(own, 3), count)
    donor, receiver = mixed[0:count // 2 * 2:2], mixed[1:count // 2 * 2:2]
    slack = jnp.minimum(tallies[donor] - 1, limit - tallies[receiver]) // 2
    slack = jnp.where((donor == sequence[0]) | (receiver == sequence[0]) | (tallies[receiver] == 0), 0, jnp.maximum(slack, 0))
    shifted = jax.random.randint(jax.random.fold_in(own, 4), (count // 2,), 0, 1 << 20) % (slack + 1)
    tallies = tallies.at[donor].add(-shifted).at[receiver].add(shifted)
    items = jnp.searchsorted(jnp.cumsum(tallies), jnp.arange(rows * top), side="right").astype(jnp.int32)
    grid = items.reshape(top, rows).T
    grid = grid[jax.random.permutation(jax.random.fold_in(own, 1), rows)]
    rotation = jax.random.randint(jax.random.fold_in(own, 2), (rows, 1), 0, top)
    return jnp.take_along_axis(grid, (jnp.arange(top)[None, :] + rotation) % top, axis=1)


def load_shares(number_of, total, bound, lean, full):
    portions = [(1 << 20) // math.isqrt(standing ** lean) + 1 for standing in range(1, number_of + 1)]
    largest = bound if full else min(bound, max(-(-total // number_of), total * portions[0] // sum(portions)))
    least = 1 if total - largest >= number_of - 1 else 0
    given, spare = [largest] + [least] * (number_of - 1), total - largest - least * (number_of - 1)
    while spare > 0:
        free = [i for i in range(1, number_of) if given[i] < largest] or [i for i in range(1, number_of) if given[i] < bound]
        whole, left = sum([portions[i] for i in free]), spare
        for i in free:
            extra = min(bound - given[i], max(1, left * portions[i] // whole), spare)
            given[i] = given[i] + extra
            spare = spare - extra
    return np.array(given)


def bell_draw(key, shape, deviation, most, shards=(), kind=jnp.bfloat16):
    entries = jax.random.normal(key, shape, jnp.float32) * deviation
    if len(shards) > 0:
        entries = block_scale(key, shape, shards, -0.22, 0.18) * entries
    return jnp.clip(entries, min=-most, max=most).astype(kind)


def setup_inputs(seed: int = 0) -> dict:
    keys = jax.random.split(jax.random.key(seed), 6)
    out_grad = bell_draw(keys[0], (TOKENS, D), 1.0, 6.0, ((0, 1024),))
    hidden_acts = bell_draw(keys[1], (TOKENS, TOP, FW), 0.04, 0.23925781, ((0, 1024),))
    gate_weights = draw_gate_weights(jax.random.fold_in(keys[5], 71), 0)
    expert_idx_keys = jax.random.split(jax.random.fold_in(keys[3], 1), TOKENS // TOK_DEV)
    expert_idx_turns = jax.random.permutation(jax.random.fold_in(keys[3], 3), TOKENS // TOK_DEV)
    expert_idx = jax.vmap(lambda own, number: deal_out(jax.random.fold_in(keys[3], 2), own, number, TOK_DEV, EXPERTS, TOP, MOST, 2))(expert_idx_keys, expert_idx_turns).reshape((TOKENS, TOP))
    down_weight = bell_draw(keys[4], (EXPERTS, FW, D), D ** -0.5, 0.09375, ((0, 64),))
    return dict(out_grad=out_grad, hidden_acts=hidden_acts, gate_weights=gate_weights, expert_idx=expert_idx, down_weight=down_weight)


def reference(out_grad, hidden_acts, gate_weights, expert_idx, down_weight):
    routed = TOKENS * TOP
    flat_expert = expert_idx.reshape(routed).astype(jnp.int32)
    row_ids = jnp.arange(routed, dtype=jnp.int32)
    group_of = (row_ids // (TOP * GROUP_TOK)).astype(jnp.int32)
    sort_keys = (flat_expert * N_DP + group_of).astype(jnp.int32)
    sorted_rows = jnp.argsort(sort_keys, stable=True).astype(jnp.int32)
    group_sizes = jnp.bincount(sort_keys, length=EXPERTS * N_DP).astype(jnp.int32)
    group_starts = (jnp.cumsum(group_sizes) - group_sizes).astype(jnp.int32)
    group_window = MOST * N_EXPERT
    padded_rows = jnp.concatenate([sorted_rows, jnp.full((group_window,), routed, jnp.int32)])
    gate_half = lax.optimization_barrier(gate_weights.astype(jnp.bfloat16)).astype(jnp.float32)
    flat_gate = jnp.concatenate([gate_half.reshape(routed), jnp.zeros((1,), jnp.float32)])
    flat_acts = jnp.concatenate([hidden_acts.reshape(routed, FW), jnp.zeros((1, FW), jnp.bfloat16)])
    grad_pad = jnp.concatenate([out_grad, jnp.zeros((1, D), jnp.bfloat16)])

    def expert_block(expert_id):
        expert_weight = down_weight[expert_id]

        def group_step(summed, group_id):
            key_now = expert_id * N_DP + group_id
            picked = lax.dynamic_slice(padded_rows, (group_starts[key_now].astype(jnp.int32),), (group_window,))
            is_live = jnp.arange(group_window, dtype=jnp.int32) < group_sizes[key_now]
            picked = jnp.where(is_live, picked, routed).astype(jnp.int32)
            token_ids = jnp.where(is_live, picked // TOP, TOKENS).astype(jnp.int32)
            grad_rows = grad_pad[token_ids]
            act_rows = flat_acts[picked]
            gate_rows = flat_gate[picked][:, None]
            grad_hidden = jnp.dot(grad_rows, expert_weight.T, preferred_element_type=jnp.float32)
            act_back = (gate_rows * grad_hidden).astype(jnp.bfloat16)
            score_back = jnp.sum(grad_hidden * act_rows.astype(jnp.float32), axis=1).astype(jnp.bfloat16)
            scaled_grad = (gate_rows * grad_rows.astype(jnp.float32)).astype(jnp.bfloat16)
            group_part = jnp.dot(act_rows.T, scaled_grad, preferred_element_type=jnp.float32).astype(jnp.bfloat16)
            return summed + group_part.astype(jnp.float32), (picked, act_back, score_back)

        summed, outputs = lax.scan(group_step, jnp.zeros((FW, D), jnp.float32), jnp.arange(N_DP, dtype=jnp.int32))
        return summed.astype(jnp.bfloat16), outputs[0], outputs[1], outputs[2]

    down_grad, picked, act_back, score_back = lax.map(expert_block, jnp.arange(EXPERTS, dtype=jnp.int32))
    target = picked.reshape(-1).astype(jnp.int32)
    act_grad = jnp.zeros((routed + 1, FW), jnp.bfloat16).at[target].set(act_back.reshape(-1, FW))[:routed]
    score = jnp.zeros((routed + 1,), jnp.float32).at[target].set(score_back.reshape(-1).astype(jnp.float32))[:routed]
    score = score.reshape(TOKENS, TOP)
    logit_grad = gate_weights * (score - jnp.sum(gate_weights * score, axis=1, keepdims=True))
    return act_grad.reshape(TOKENS, TOP, FW), logit_grad, down_grad
```

```python
import jax
import jax.numpy as jnp
from jax import lax
from jax.experimental import pallas as pl
from jax.experimental.pallas import tpu as pltpu
from jax.sharding import Mesh
from jax.sharding import PartitionSpec as P

MOST = 3
CORES = 2
X, Y, Z = 4, 8, 16
BF16 = jnp.bfloat16
F32 = jnp.float32


def weight_kernel(left_own, left_pair, rows_own, rows_pair, out):
    total = jnp.dot(left_own[...], rows_own[...], preferred_element_type=F32)
    total = total + jnp.dot(left_pair[...], rows_pair[...], preferred_element_type=F32)
    out[...] = total.astype(out.dtype)


def weight_term(left_own, left_pair, rows_own, rows_pair):
    half, slots = left_own.shape
    width = rows_own.shape[1]
    block = 1024
    return pl.pallas_call(
        weight_kernel,
        grid=(width // block,),
        out_shape=jax.ShapeDtypeStruct((half, width), BF16),
        in_specs=[
            pl.BlockSpec((half, slots), lambda i: (0, 0)),
            pl.BlockSpec((half, slots), lambda i: (0, 0)),
            pl.BlockSpec((slots, block), lambda i: (0, i)),
            pl.BlockSpec((slots, block), lambda i: (0, i)),
        ],
        out_specs=pl.BlockSpec((half, block), lambda i: (0, i)),
        compiler_params=pltpu.CompilerParams(vmem_limit_bytes=32 * 1024 * 1024),
        cost_estimate=pl.CostEstimate(
            flops=4 * half * slots * width,
            bytes_accessed=2 * (2 * slots * width + half * width + 2 * half * slots),
            transcendentals=0,
        ),
        name="weight_term",
    )(left_own, left_pair, rows_own, rows_pair)


def shards(out_grad, hidden_acts, gate_weights, expert_idx, down_weight):
    tok_rows, top_count = expert_idx.shape
    routed = tok_rows * top_count
    hidden = hidden_acts.shape[2]
    half = hidden // CORES
    experts = X * Z
    slot_count = experts * MOST
    core = lax.axis_index("core")
    z_at = lax.axis_index("z")

    column = lax.all_gather(out_grad, "z", axis=0, tiled=True)

    flat_expert = expert_idx.reshape(routed)
    member = (flat_expert[:, None] == jnp.arange(experts, dtype=jnp.int32)[None, :]).astype(BF16)
    row_line = jnp.arange(routed, dtype=jnp.int32)
    earlier_mask = (row_line[:, None] > row_line[None, :]).astype(BF16)
    earlier = jnp.dot(earlier_mask, member, preferred_element_type=F32)
    position = jnp.sum(earlier * member.astype(F32), axis=1).astype(jnp.int32)
    slot_index = flat_expert * MOST + position
    taken = jnp.arange(slot_count, dtype=jnp.int32)[:, None] == slot_index[None, :]
    placement = taken.astype(BF16)

    token_of = (z_at * tok_rows + row_line // top_count).astype(F32)
    slot_token = jnp.sum(jnp.where(taken, token_of[None, :] + 1.0, 0.0), axis=1) - 1.0
    slot_token = lax.all_to_all(
        slot_token.reshape(X, Z, MOST), "z", split_axis=1, concat_axis=1, tiled=True
    )

    gate_half = lax.optimization_barrier(gate_weights.astype(BF16)).astype(F32)
    flat_acts = hidden_acts.reshape(routed, hidden).astype(F32)
    gated = (gate_half.reshape(routed, 1) * flat_acts).astype(BF16)
    send_acts = jnp.dot(placement, gated, preferred_element_type=F32).astype(BF16)
    acts_in = lax.all_to_all(
        send_acts.reshape(experts, MOST, hidden),
        ("x", "z"),
        split_axis=0,
        concat_axis=0,
        tiled=True,
    ).reshape(slot_count, hidden)

    line = jnp.arange(hidden, dtype=jnp.int32)
    piece = hidden // (Y * CORES)
    unit = ((line % half) // piece * CORES + line // half) * piece + line % piece
    reorder = (unit[:, None] == line[None, :]).astype(BF16)
    left = lax.dot_general(
        reorder, acts_in, (((1,), (1,)), ((), ())), preferred_element_type=F32
    ).astype(BF16)
    left_own = lax.dynamic_slice_in_dim(left, core * half, half, 0)
    left_away = lax.dynamic_slice_in_dim(left, (1 - core) * half, half, 0)
    swap = [(0, 1), (1, 0)]
    left_pair = lax.ppermute(left_away, "core", swap)

    pick = (
        slot_token.reshape(slot_count, 1)
        == jnp.arange(Z * tok_rows, dtype=jnp.int32)[None, :].astype(F32)
    ).astype(BF16)
    picked = jnp.dot(pick, column, preferred_element_type=F32).astype(BF16)
    rows = lax.all_to_all(
        picked.reshape(X, Z * MOST, picked.shape[1]),
        "x",
        split_axis=0,
        concat_axis=0,
        tiled=True,
    ).reshape(slot_count, picked.shape[1])
    rows_pair = lax.ppermute(rows, "core", swap)

    weight_part = weight_term(left_own, left_pair, rows, rows_pair)
    summed = lax.psum_scatter(weight_part, "y", scatter_dimension=0, tiled=True)

    grad_hidden = lax.dot_general(
        rows, down_weight[0], (((1,), (1,)), ((), ())), preferred_element_type=F32
    ).astype(BF16)
    back = lax.all_to_all(
        grad_hidden.reshape(experts, MOST, hidden),
        ("x", "z"),
        split_axis=0,
        concat_axis=0,
        tiled=True,
    ).reshape(slot_count, hidden)
    grad_tok = lax.dot_general(
        placement, back, (((0,), (0,)), ((), ())), preferred_element_type=F32
    )
    act_grad = (gate_half.reshape(routed, 1) * grad_tok).astype(BF16)
    score = jnp.sum(grad_tok * flat_acts, axis=1).astype(BF16).astype(F32)
    score = score.reshape(tok_rows, top_count)
    logit_grad = gate_weights * (score - jnp.sum(gate_weights * score, axis=1, keepdims=True))
    return act_grad.reshape(tok_rows, top_count, hidden), logit_grad, summed[None]


def solution(mesh):
    dims = Mesh(mesh.devices.reshape(Y, CORES, X, Z), ("y", "core", "x", "z"))
    tokens = ("y", "core", "x", "z")
    return jax.shard_map(
        shards,
        mesh=dims,
        in_specs=(
            P(tokens, None),
            P(tokens, None, None),
            P(tokens, None),
            P(tokens, None),
            P(("x", "z"), None, None),
        ),
        out_specs=(
            P(tokens, None, None),
            P(tokens, None),
            P(("x", "z"), ("y", "core"), None),
        ),
        check_vma=False,
    )
```

```python
import functools

import jax
import jax.numpy as jnp
from jax import lax
from jax.experimental import pallas as pl
from jax.experimental.pallas import tpu as pltpu
from jax.sharding import Mesh
from jax.sharding import PartitionSpec as P

MOST = 3
CORES = 2
X, Y, Z = 4, 8, 16
LANES = 128
EARLY = 1536
BLOCK = 512
BF16 = jnp.bfloat16
F32 = jnp.float32
ROOM = 32 * 1024 * 1024


def pick_kernel(pick, column, after, out):
    del after
    out[...] = jnp.dot(pick[...], column[...], preferred_element_type=F32).astype(out.dtype)


def pick_rows(pick, column, width, after):
    slots, tokens = pick.shape
    return pl.pallas_call(
        pick_kernel,
        grid=(width // BLOCK,),
        out_shape=jax.ShapeDtypeStruct((slots, width), BF16),
        in_specs=[
            pl.BlockSpec((slots, tokens), lambda i: (0, 0)),
            pl.BlockSpec((tokens, BLOCK), lambda i: (0, i)),
            pl.BlockSpec(memory_space=pl.ANY),
        ],
        out_specs=pl.BlockSpec((slots, BLOCK), lambda i: (0, i)),
        compiler_params=pltpu.CompilerParams(vmem_limit_bytes=ROOM),
        cost_estimate=pl.CostEstimate(
            flops=2 * slots * tokens * width,
            bytes_accessed=2 * width * (slots + tokens),
            transcendentals=0,
        ),
        name="pick_rows",
    )(pick, column, after)


def weight_kernel(left_own, left_pair, rows_own, rows_pair, *rest):
    out = rest[-1]
    total = jnp.dot(left_own[...], rows_own[...], preferred_element_type=F32)
    total = total + jnp.dot(left_pair[...], rows_pair[...], preferred_element_type=F32)
    out[...] = total.astype(out.dtype)


def weight_term(left_own, left_pair, rows_own, rows_pair, full, start, into):
    half, slots = left_own.shape
    width = rows_own.shape[1]
    first = start // BLOCK
    operands = [left_own, left_pair, rows_own, rows_pair]
    in_specs = [
        pl.BlockSpec((half, slots), lambda i: (0, 0)),
        pl.BlockSpec((half, slots), lambda i: (0, 0)),
        pl.BlockSpec((slots, BLOCK), lambda i: (0, i)),
        pl.BlockSpec((slots, BLOCK), lambda i: (0, i)),
    ]
    aliases = {}
    if into is not None:
        operands.append(into)
        in_specs.append(pl.BlockSpec(memory_space=pl.ANY))
        aliases = {4: 0}
    return pl.pallas_call(
        weight_kernel,
        grid=(width // BLOCK,),
        out_shape=jax.ShapeDtypeStruct((half, full), BF16),
        in_specs=in_specs,
        out_specs=pl.BlockSpec((half, BLOCK), lambda i: (0, i + first)),
        input_output_aliases=aliases,
        compiler_params=pltpu.CompilerParams(vmem_limit_bytes=ROOM),
        cost_estimate=pl.CostEstimate(
            flops=4 * half * slots * width,
            bytes_accessed=2 * (2 * slots * width + half * width + 2 * half * slots),
            transcendentals=0,
        ),
        name="weight_term",
    )(*operands)


def hidden_kernel(early_steps, rows_early, rows_late, weight, out, total):
    step = pl.program_id(0)

    @pl.when(step == 0)
    def _():
        total[...] = jnp.zeros_like(total)

    def add(rows):
        total[...] += lax.dot_general(
            rows[...], weight[...], (((1,), (1,)), ((), ())), preferred_element_type=F32
        )

    @pl.when(step < early_steps)
    def _():
        add(rows_early)

    @pl.when(step >= early_steps)
    def _():
        add(rows_late)

    @pl.when(step == pl.num_programs(0) - 1)
    def _():
        out[...] = total[...].astype(out.dtype)


def hidden_term(rows_early, rows_late, weight):
    slots = rows_early.shape[0]
    hidden, width = weight.shape[1:]
    early = rows_early.shape[1] // BLOCK
    return pl.pallas_call(
        functools.partial(hidden_kernel, early),
        grid=(width // BLOCK,),
        out_shape=jax.ShapeDtypeStruct((slots, hidden), BF16),
        in_specs=[
            pl.BlockSpec((slots, BLOCK), lambda i: (0, jnp.minimum(i, early - 1))),
            pl.BlockSpec((slots, BLOCK), lambda i: (0, jnp.maximum(i - early, 0))),
            pl.BlockSpec((None, hidden, BLOCK), lambda i: (0, 0, i)),
        ],
        out_specs=pl.BlockSpec((slots, hidden), lambda i: (0, 0)),
        scratch_shapes=[pltpu.VMEM((slots, hidden), F32)],
        compiler_params=pltpu.CompilerParams(vmem_limit_bytes=ROOM),
        cost_estimate=pl.CostEstimate(
            flops=2 * slots * hidden * width,
            bytes_accessed=2 * (slots * width + hidden * width + slots * hidden),
            transcendentals=0,
        ),
        name="hidden_term",
    )(rows_early, rows_late, weight)


def shards(out_grad, hidden_acts, gate_weights, expert_idx, down_weight):
    tok_rows, top_count = expert_idx.shape
    routed = tok_rows * top_count
    width = out_grad.shape[1]
    hidden = hidden_acts.shape[2]
    half = hidden // CORES
    experts = X * Z
    slot_count = experts * MOST
    core = lax.axis_index("core")
    z_at = lax.axis_index("z")
    swap = [(0, 1), (1, 0)]

    column_late = lax.all_gather(out_grad[:, EARLY:], "z", axis=0, tiled=True)

    flat_expert = expert_idx.reshape(routed)
    member = (flat_expert[:, None] == jnp.arange(experts, dtype=jnp.int32)[None, :]).astype(BF16)
    row_line = jnp.arange(routed, dtype=jnp.int32)
    earlier_mask = (row_line[:, None] > row_line[None, :]).astype(BF16)
    earlier = jnp.dot(earlier_mask, member, preferred_element_type=F32)
    position = jnp.sum(earlier * member.astype(F32), axis=1).astype(jnp.int32)
    slot_index = flat_expert * MOST + position
    placement = (jnp.arange(slot_count, dtype=jnp.int32)[:, None] == slot_index[None, :]).astype(BF16)

    plane_of = (jnp.arange(Z, dtype=jnp.int32)[:, None] == (flat_expert % Z)[None, :]).astype(BF16)
    slot_of = (flat_expert // Z) * MOST + position
    token_of = (row_line // top_count + 1).astype(F32)
    token_at = jnp.where(
        slot_of[:, None] == jnp.arange(LANES, dtype=jnp.int32)[None, :], token_of[:, None], 0.0
    ).astype(BF16)
    table = jnp.dot(plane_of, token_at, preferred_element_type=F32).astype(BF16)

    gate_half = lax.optimization_barrier(gate_weights.astype(BF16)).astype(F32)
    flat_acts = hidden_acts.reshape(routed, hidden).astype(F32)
    gated = (gate_half.reshape(routed, 1) * flat_acts).astype(BF16)
    send_acts = jnp.dot(placement, gated, preferred_element_type=F32).astype(BF16)
    acts_in = lax.all_to_all(
        send_acts.reshape(experts, MOST, hidden),
        ("x", "z"),
        split_axis=0,
        concat_axis=0,
        tiled=True,
    ).reshape(slot_count, hidden)

    line = jnp.arange(hidden, dtype=jnp.int32)
    piece = hidden // (Y * CORES)
    unit = ((line % half) // piece * CORES + line // half) * piece + line % piece
    reorder = (unit[:, None] == line[None, :]).astype(BF16)
    left = lax.dot_general(
        reorder, acts_in, (((1,), (1,)), ((), ())), preferred_element_type=F32
    ).astype(BF16)
    left_own = lax.dynamic_slice_in_dim(left, core * half, half, 0)
    left_away = lax.dynamic_slice_in_dim(left, (1 - core) * half, half, 0)
    left_pair = lax.ppermute(left_away, "core", swap)

    column_early = lax.all_gather(
        jnp.concatenate([out_grad[:, :EARLY], table], axis=1), "z", axis=0, tiled=True
    )
    tables = column_early[:, EARLY : EARLY + X * MOST].reshape(Z, Z, X, MOST)
    mine = lax.dynamic_slice_in_dim(tables, z_at, 1, 1).reshape(Z, X, MOST).astype(F32)
    base = (jnp.arange(Z, dtype=jnp.int32) * tok_rows).astype(F32)
    token = jnp.where(mine > 0.0, mine - 1.0 + base[:, None, None], -1.0)
    token = jnp.transpose(token, (1, 0, 2)).reshape(slot_count, 1)
    pick = (token == jnp.arange(Z * tok_rows, dtype=jnp.int32)[None, :].astype(F32)).astype(BF16)

    def rows_of(column, columns, after):
        picked = pick_rows(pick, column, columns, after)
        return lax.all_to_all(
            picked.reshape(X, Z * MOST, columns), "x", split_axis=0, concat_axis=0, tiled=True
        ).reshape(slot_count, columns)

    rows_early = rows_of(column_early, EARLY, left_own)
    pair_early = lax.ppermute(rows_early, "core", swap)
    part = weight_term(left_own, left_pair, rows_early, pair_early, width, 0, None)
    rows_late = rows_of(column_late, width - EARLY, part)
    pair_late = lax.ppermute(rows_late, "core", swap)
    part = weight_term(left_own, left_pair, rows_late, pair_late, width, EARLY, part)
    summed = lax.psum_scatter(part, "y", scatter_dimension=0, tiled=True)

    grad_hidden = hidden_term(rows_early, rows_late, down_weight)
    back = lax.all_to_all(
        grad_hidden.reshape(experts, MOST, hidden),
        ("x", "z"),
        split_axis=0,
        concat_axis=0,
        tiled=True,
    ).reshape(slot_count, hidden)
    grad_tok = lax.dot_general(
        placement, back, (((0,), (0,)), ((), ())), preferred_element_type=F32
    )
    act_grad = (gate_half.reshape(routed, 1) * grad_tok).astype(BF16)
    score = jnp.sum(grad_tok * flat_acts, axis=1).astype(BF16).astype(F32)
    score = score.reshape(tok_rows, top_count)
    logit_grad = gate_weights * (score - jnp.sum(gate_weights * score, axis=1, keepdims=True))
    return act_grad.reshape(tok_rows, top_count, hidden), logit_grad, summed[None]


def solution(mesh):
    dims = Mesh(mesh.devices.reshape(Y, CORES, X, Z), ("y", "core", "x", "z"))
    tokens = ("y", "core", "x", "z")
    return jax.shard_map(
        shards,
        mesh=dims,
        in_specs=(
            P(tokens, None),
            P(tokens, None, None),
            P(tokens, None),
            P(tokens, None),
            P(("x", "z"), None, None),
        ),
        out_specs=(
            P(tokens, None, None),
            P(tokens, None),
            P(("x", "z"), ("y", "core"), None),
        ),
        check_vma=False,
    )
```

```python
import jax
import jax.numpy as jnp
from jax import lax
from jax.experimental import pallas as pl
from jax.experimental.pallas import tpu as pltpu
from jax.sharding import Mesh
from jax.sharding import PartitionSpec as P

MOST = 3
CORES = 2
X, Y, Z = 4, 8, 16
BLOCK = 1024
BF16 = jnp.bfloat16
F32 = jnp.float32
MIB = 1024 * 1024


def pick_kernel(pick, column, after, out):
    del after
    out[...] = jnp.dot(pick[...], column[...], preferred_element_type=F32).astype(out.dtype)


def pick_rows(pick, column, after):
    slots, tokens = pick.shape
    width = column.shape[1]
    return pl.pallas_call(
        pick_kernel,
        grid=(width // BLOCK,),
        out_shape=jax.ShapeDtypeStruct((slots, width), BF16),
        in_specs=[
            pl.BlockSpec((slots, tokens), lambda i: (0, 0)),
            pl.BlockSpec((tokens, BLOCK), lambda i: (0, i)),
            pl.BlockSpec(memory_space=pl.ANY),
        ],
        out_specs=pl.BlockSpec((slots, BLOCK), lambda i: (0, i)),
        compiler_params=pltpu.CompilerParams(vmem_limit_bytes=60 * MIB),
        cost_estimate=pl.CostEstimate(
            flops=2 * slots * tokens * width,
            bytes_accessed=2 * width * (slots + tokens),
            transcendentals=0,
        ),
        name="pick_rows",
    )(pick, column, after)


def weight_kernel(left_own, left_pair, rows_own, rows_pair, out):
    total = jnp.dot(left_own[...], rows_own[...], preferred_element_type=F32)
    total = total + jnp.dot(left_pair[...], rows_pair[...], preferred_element_type=F32)
    out[...] = total.astype(out.dtype)


def weight_term(left_own, left_pair, rows_own, rows_pair):
    half, slots = left_own.shape
    width = rows_own.shape[1]
    return pl.pallas_call(
        weight_kernel,
        grid=(width // BLOCK,),
        out_shape=jax.ShapeDtypeStruct((half, width), BF16),
        in_specs=[
            pl.BlockSpec((half, slots), lambda i: (0, 0)),
            pl.BlockSpec((half, slots), lambda i: (0, 0)),
            pl.BlockSpec((slots, BLOCK), lambda i: (0, i)),
            pl.BlockSpec((slots, BLOCK), lambda i: (0, i)),
        ],
        out_specs=pl.BlockSpec((half, BLOCK), lambda i: (0, i)),
        compiler_params=pltpu.CompilerParams(vmem_limit_bytes=49 * MIB),
        cost_estimate=pl.CostEstimate(
            flops=4 * half * slots * width,
            bytes_accessed=2 * (2 * slots * width + half * width + 2 * half * slots),
            transcendentals=0,
        ),
        name="weight_term",
    )(left_own, left_pair, rows_own, rows_pair)


def hidden_kernel(rows, weight, out, total):
    step = pl.program_id(0)

    @pl.when(step == 0)
    def _():
        total[...] = jnp.zeros_like(total)

    total[...] += lax.dot_general(
        rows[...], weight[...], (((1,), (1,)), ((), ())), preferred_element_type=F32
    )

    @pl.when(step == pl.num_programs(0) - 1)
    def _():
        out[...] = total[...].astype(out.dtype)


def hidden_term(rows, weight):
    slots = rows.shape[0]
    hidden, width = weight.shape[1:]
    return pl.pallas_call(
        hidden_kernel,
        grid=(width // BLOCK,),
        out_shape=jax.ShapeDtypeStruct((slots, hidden), BF16),
        in_specs=[
            pl.BlockSpec((slots, BLOCK), lambda i: (0, i)),
            pl.BlockSpec((None, hidden, BLOCK), lambda i: (0, 0, i)),
        ],
        out_specs=pl.BlockSpec((slots, hidden), lambda i: (0, 0)),
        scratch_shapes=[pltpu.VMEM((slots, hidden), F32)],
        compiler_params=pltpu.CompilerParams(vmem_limit_bytes=49 * MIB),
        cost_estimate=pl.CostEstimate(
            flops=2 * slots * hidden * width,
            bytes_accessed=2 * (slots * width + hidden * width + slots * hidden),
            transcendentals=0,
        ),
        name="hidden_term",
    )(rows, weight)


def shards(out_grad, hidden_acts, gate_weights, expert_idx, down_weight):
    tok_rows, top_count = expert_idx.shape
    routed = tok_rows * top_count
    width = out_grad.shape[1]
    hidden = hidden_acts.shape[2]
    half = hidden // CORES
    experts = X * Z
    slot_count = experts * MOST
    core = lax.axis_index("core")
    z_at = lax.axis_index("z")
    swap = [(0, 1), (1, 0)]

    column = lax.all_gather(out_grad, "z", axis=0, tiled=True)

    flat_expert = expert_idx.reshape(routed)
    member = (flat_expert[:, None] == jnp.arange(experts, dtype=jnp.int32)[None, :]).astype(BF16)
    row_line = jnp.arange(routed, dtype=jnp.int32)
    earlier_mask = (row_line[:, None] > row_line[None, :]).astype(BF16)
    earlier = jnp.dot(earlier_mask, member, preferred_element_type=F32)
    position = jnp.sum(earlier * member.astype(F32), axis=1).astype(jnp.int32)
    slot_index = flat_expert * MOST + position
    placement = (jnp.arange(slot_count, dtype=jnp.int32)[:, None] == slot_index[None, :]).astype(BF16)

    taken = jnp.arange(slot_count, dtype=jnp.int32)[:, None] == slot_index[None, :]
    token_of = (z_at * tok_rows + row_line // top_count).astype(F32)
    token = jnp.sum(jnp.where(taken, token_of[None, :] + 1.0, 0.0), axis=1) - 1.0
    token = lax.all_to_all(
        token.reshape(X, Z, MOST), "z", split_axis=1, concat_axis=1, tiled=True
    ).reshape(slot_count, 1)
    pick = (token == jnp.arange(Z * tok_rows, dtype=jnp.int32)[None, :].astype(F32)).astype(BF16)

    gate_half = lax.optimization_barrier(gate_weights.astype(BF16)).astype(F32)
    flat_acts = hidden_acts.reshape(routed, hidden).astype(F32)
    gated = (gate_half.reshape(routed, 1) * flat_acts).astype(BF16)
    send_acts = jnp.dot(placement, gated, preferred_element_type=F32).astype(BF16)
    acts_in = lax.all_to_all(
        send_acts.reshape(experts, MOST, hidden),
        ("x", "z"),
        split_axis=0,
        concat_axis=0,
        tiled=True,
    ).reshape(slot_count, hidden)

    line = jnp.arange(hidden, dtype=jnp.int32)
    piece = hidden // (Y * CORES)
    unit = ((line % half) // piece * CORES + line // half) * piece + line % piece
    reorder = (unit[:, None] == line[None, :]).astype(BF16)
    left = lax.dot_general(
        reorder, acts_in, (((1,), (1,)), ((), ())), preferred_element_type=F32
    ).astype(BF16)
    left_own = lax.dynamic_slice_in_dim(left, core * half, half, 0)
    left_away = lax.dynamic_slice_in_dim(left, (1 - core) * half, half, 0)

    picked = pick_rows(pick, column, acts_in)
    rows = lax.all_to_all(
        picked.reshape(X, Z * MOST, width), "x", split_axis=0, concat_axis=0, tiled=True
    ).reshape(slot_count, width)
    rows, left_own, left_away = lax.optimization_barrier((rows, left_own, left_away))
    left_pair = lax.ppermute(left_away, "core", swap)
    rows_pair = lax.ppermute(rows, "core", swap)

    part = weight_term(left_own, left_pair, rows, rows_pair)
    summed = lax.psum_scatter(part, "y", scatter_dimension=0, tiled=True)

    grad_hidden = hidden_term(rows, down_weight)
    back = lax.all_to_all(
        grad_hidden.reshape(experts, MOST, hidden),
        ("x", "z"),
        split_axis=0,
        concat_axis=0,
        tiled=True,
    ).reshape(slot_count, hidden)
    grad_tok = lax.dot_general(
        placement, back, (((0,), (0,)), ((), ())), preferred_element_type=F32
    )
    act_grad = (gate_half.reshape(routed, 1) * grad_tok).astype(BF16)
    score = jnp.sum(grad_tok * flat_acts, axis=1).astype(BF16).astype(F32)
    score = score.reshape(tok_rows, top_count)
    logit_grad = gate_weights * (score - jnp.sum(gate_weights * score, axis=1, keepdims=True))
    return act_grad.reshape(tok_rows, top_count, hidden), logit_grad, summed[None]


def solution(mesh):
    dims = Mesh(mesh.devices.reshape(Y, CORES, X, Z), ("y", "core", "x", "z"))
    tokens = ("y", "core", "x", "z")
    return jax.shard_map(
        shards,
        mesh=dims,
        in_specs=(
            P(tokens, None),
            P(tokens, None, None),
            P(tokens, None),
            P(tokens, None),
            P(("x", "z"), None, None),
        ),
        out_specs=(
            P(tokens, None, None),
            P(tokens, None),
            P(("x", "z"), ("y", "core"), None),
        ),
        check_vma=False,
    )
```

```python
import jax
import jax.numpy as jnp
from jax import lax
from jax.experimental import pallas as pl
from jax.experimental.pallas import tpu as pltpu
from jax.sharding import Mesh
from jax.sharding import PartitionSpec as P

MOST = 3
TOK = 16
CORES = 2
X, Y, ZH, ZL = 4, 8, 4, 4
Z = ZH * ZL
LANES = 128
BLOCK = 1024
BF16 = jnp.bfloat16
F32 = jnp.float32
MIB = 1024 * 1024


def pick_kernel(home, lane, *refs):
    blocks, tables, (after, out, pick) = refs[:5], refs[5:10], refs[10:]
    del after
    slots, tokens = pick.shape

    @pl.when(pl.program_id(0) == 0)
    def _():
        at = lax.broadcasted_iota(jnp.int32, (slots, tokens), 1)
        line = jnp.where(at == home[...], 1.0, 0.0).astype(BF16)
        table = jnp.concatenate([ref[...] for ref in tables], axis=0)
        values = jnp.dot(line, table, preferred_element_type=F32)
        lanes = lax.broadcasted_iota(jnp.int32, values.shape, 1)
        value = jnp.sum(jnp.where(lanes == lane[...], values, 0.0), axis=1, keepdims=True)
        first = home[...] // TOK * TOK
        token = jnp.where(value > 0.0, value.astype(jnp.int32) - 1 + first, -1)
        pick[...] = jnp.where(at == token, 1.0, 0.0).astype(pick.dtype)

    held = jnp.concatenate([ref[...] for ref in blocks], axis=0)
    out[...] = jnp.dot(pick[...], held, preferred_element_type=F32).astype(out.dtype)


def pick_rows(home, lane, blocks, width, after):
    slots = home.shape[0]
    tokens = sum(block.shape[0] for block in blocks)
    last = width // LANES
    return pl.pallas_call(
        pick_kernel,
        grid=(width // BLOCK,),
        out_shape=jax.ShapeDtypeStruct((slots, width), BF16),
        in_specs=[pl.BlockSpec((slots, 1), lambda i: (0, 0))] * 2
        + [pl.BlockSpec((block.shape[0], BLOCK), lambda i: (0, i)) for block in blocks]
        + [pl.BlockSpec((block.shape[0], LANES), lambda i: (0, last)) for block in blocks]
        + [pl.BlockSpec(memory_space=pl.ANY)],
        out_specs=pl.BlockSpec((slots, BLOCK), lambda i: (0, i)),
        scratch_shapes=[pltpu.VMEM((slots, tokens), BF16)],
        compiler_params=pltpu.CompilerParams(vmem_limit_bytes=49 * MIB),
        cost_estimate=pl.CostEstimate(
            flops=2 * slots * tokens * width,
            bytes_accessed=2 * width * (slots + tokens),
            transcendentals=0,
        ),
        name="pick_rows",
    )(home, lane, *blocks, *blocks, after)


def weight_kernel(left_own, left_pair, rows_own, rows_pair, out):
    total = jnp.dot(left_own[...], rows_own[...], preferred_element_type=F32)
    total = total + jnp.dot(left_pair[...], rows_pair[...], preferred_element_type=F32)
    out[...] = total.astype(out.dtype)


def weight_term(left_own, left_pair, rows_own, rows_pair):
    half, slots = left_own.shape
    width = rows_own.shape[1]
    return pl.pallas_call(
        weight_kernel,
        grid=(width // BLOCK,),
        out_shape=jax.ShapeDtypeStruct((half, width), BF16),
        in_specs=[
            pl.BlockSpec((half, slots), lambda i: (0, 0)),
            pl.BlockSpec((half, slots), lambda i: (0, 0)),
            pl.BlockSpec((slots, BLOCK), lambda i: (0, i)),
            pl.BlockSpec((slots, BLOCK), lambda i: (0, i)),
        ],
        out_specs=pl.BlockSpec((half, BLOCK), lambda i: (0, i)),
        compiler_params=pltpu.CompilerParams(vmem_limit_bytes=49 * MIB),
        cost_estimate=pl.CostEstimate(
            flops=4 * half * slots * width,
            bytes_accessed=2 * (2 * slots * width + half * width + 2 * half * slots),
            transcendentals=0,
        ),
        name="weight_term",
    )(left_own, left_pair, rows_own, rows_pair)


def hidden_kernel(rows, weight, order, out, total):
    step = pl.program_id(0)

    @pl.when(step == 0)
    def _():
        total[...] = jnp.zeros_like(total)

    total[...] += lax.dot_general(
        rows[...], weight[...], (((1,), (1,)), ((), ())), preferred_element_type=F32
    )

    @pl.when(step == pl.num_programs(0) - 1)
    def _():
        rounded = total[...].astype(BF16)
        out[...] = jnp.dot(order[...], rounded, preferred_element_type=F32).astype(out.dtype)


def hidden_term(rows, weight, order):
    slots = rows.shape[0]
    hidden, width = weight.shape[1:]
    return pl.pallas_call(
        hidden_kernel,
        grid=(width // BLOCK,),
        out_shape=jax.ShapeDtypeStruct((slots, hidden), BF16),
        in_specs=[
            pl.BlockSpec((slots, BLOCK), lambda i: (0, i)),
            pl.BlockSpec((None, hidden, BLOCK), lambda i: (0, 0, i)),
            pl.BlockSpec((slots, slots), lambda i: (0, 0)),
        ],
        out_specs=pl.BlockSpec((slots, hidden), lambda i: (0, 0)),
        scratch_shapes=[pltpu.VMEM((slots, hidden), F32)],
        compiler_params=pltpu.CompilerParams(vmem_limit_bytes=49 * MIB),
        cost_estimate=pl.CostEstimate(
            flops=2 * slots * hidden * width,
            bytes_accessed=2 * (slots * width + hidden * width + slots * hidden),
            transcendentals=0,
        ),
        name="hidden_term",
    )(rows, weight, order)


def shards(out_grad, hidden_acts, gate_weights, expert_idx, down_weight):
    tok_rows, top_count = expert_idx.shape
    routed = tok_rows * top_count
    width = out_grad.shape[1]
    hidden = hidden_acts.shape[2]
    half = hidden // CORES
    experts = X * Z
    slot_count = experts * MOST
    core = lax.axis_index("core")
    planes = ("zh", "zl")
    z_at = lax.axis_index(planes)
    swap = [(0, 1), (1, 0)]

    flat_expert = expert_idx.reshape(routed)
    member = (flat_expert[:, None] == jnp.arange(experts, dtype=jnp.int32)[None, :]).astype(BF16)
    row_line = jnp.arange(routed, dtype=jnp.int32)
    earlier_mask = (row_line[:, None] > row_line[None, :]).astype(BF16)
    earlier = jnp.dot(earlier_mask, member, preferred_element_type=F32)
    position = jnp.sum(earlier * member.astype(F32), axis=1).astype(jnp.int32)
    slot_index = flat_expert * MOST + position
    placement = (jnp.arange(slot_count, dtype=jnp.int32)[:, None] == slot_index[None, :]).astype(BF16)

    plane_of = (jnp.arange(Z, dtype=jnp.int32)[:, None] == (flat_expert % Z)[None, :]).astype(BF16)
    lane_of = (flat_expert // Z) * MOST + position
    token_of = (row_line // top_count + 1).astype(F32)
    token_at = jnp.where(
        lane_of[:, None] == jnp.arange(LANES, dtype=jnp.int32)[None, :], token_of[:, None], 0.0
    ).astype(BF16)
    table = jnp.dot(plane_of, token_at, preferred_element_type=F32).astype(BF16)

    own = lax.all_gather(jnp.concatenate([out_grad, table], axis=1), "zh", axis=0, tiled=True)

    def shifted(part, by):
        return lax.ppermute(part, planes, [(i, (i + by) % Z) for i in range(Z)])

    middle = own.shape[0] // 2
    blocks = (
        own,
        shifted(own, -1),
        shifted(own, 1),
        shifted(own[:middle], 2),
        shifted(own[middle:], -2),
    )

    gate_half = lax.optimization_barrier(gate_weights.astype(BF16)).astype(F32)
    flat_acts = hidden_acts.reshape(routed, hidden).astype(F32)
    gated = (gate_half.reshape(routed, 1) * flat_acts).astype(BF16)
    send_acts = jnp.dot(placement, gated, preferred_element_type=F32).astype(BF16)
    acts_in = lax.all_to_all(
        send_acts.reshape(experts, MOST, hidden),
        ("x",) + planes,
        split_axis=0,
        concat_axis=0,
        tiled=True,
    ).reshape(slot_count, hidden)

    slot = jnp.arange(slot_count, dtype=jnp.int32)
    per_x = Z * MOST
    held, high, rank = slot // (ZH * MOST) % ZL, slot // MOST % ZH, slot % MOST
    turn = jnp.where(held == 1, 1, jnp.where(held == 2, ZL - 1, jnp.where(held == 3, 2, 0)))
    source = high * ZL + (z_at + turn) % ZL
    home_slot = slot // per_x * per_x + source * MOST + rank
    order = (slot[:, None] == home_slot[None, :]).astype(BF16)

    line = jnp.arange(hidden, dtype=jnp.int32)
    piece = hidden // (Y * CORES)
    unit = ((line % half) // piece * CORES + line // half) * piece + line % piece
    reorder = (unit[:, None] == line[None, :]).astype(BF16)
    acts_rows = lax.dot_general(
        order, acts_in, (((0,), (0,)), ((), ())), preferred_element_type=F32
    ).astype(BF16)
    left = lax.dot_general(
        reorder, acts_rows, (((1,), (1,)), ((), ())), preferred_element_type=F32
    ).astype(BF16)
    left_own = lax.dynamic_slice_in_dim(left, core * half, half, 0)
    left_away = lax.dynamic_slice_in_dim(left, (1 - core) * half, half, 0)

    home = (held * ZH + high) * tok_rows + z_at
    lane = slot // per_x * MOST + rank
    picked = pick_rows(home[:, None], lane[:, None], blocks, width, acts_in)
    rows = lax.all_to_all(
        picked.reshape(X, Z * MOST, width), "x", split_axis=0, concat_axis=0, tiled=True
    ).reshape(slot_count, width)
    rows, left_own, left_away = lax.optimization_barrier((rows, left_own, left_away))
    left_pair = lax.ppermute(left_away, "core", swap)
    rows_pair = lax.ppermute(rows, "core", swap)

    part = weight_term(left_own, left_pair, rows, rows_pair)
    summed = lax.psum_scatter(part, "y", scatter_dimension=0, tiled=True)

    grad_hidden = hidden_term(rows, down_weight, order)
    back = lax.all_to_all(
        grad_hidden.reshape(experts, MOST, hidden),
        ("x",) + planes,
        split_axis=0,
        concat_axis=0,
        tiled=True,
    ).reshape(slot_count, hidden)
    grad_tok = lax.dot_general(
        placement, back, (((0,), (0,)), ((), ())), preferred_element_type=F32
    )
    act_grad = (gate_half.reshape(routed, 1) * grad_tok).astype(BF16)
    score = jnp.sum(grad_tok * flat_acts, axis=1).astype(BF16).astype(F32)
    score = score.reshape(tok_rows, top_count)
    logit_grad = gate_weights * (score - jnp.sum(gate_weights * score, axis=1, keepdims=True))
    return act_grad.reshape(tok_rows, top_count, hidden), logit_grad, summed[None]


def solution(mesh):
    dims = Mesh(mesh.devices.reshape(Y, CORES, X, ZH, ZL), ("y", "core", "x", "zh", "zl"))
    experts = ("x", "zh", "zl")
    tokens = ("y", "core") + experts
    return jax.shard_map(
        shards,
        mesh=dims,
        in_specs=(
            P(tokens, None),
            P(tokens, None, None),
            P(tokens, None),
            P(tokens, None),
            P(experts, None, None),
        ),
        out_specs=(
            P(tokens, None, None),
            P(tokens, None),
            P(experts, ("y", "core"), None),
        ),
        check_vma=False,
    )
```

```python
import jax
import jax.numpy as jnp
from jax import lax
from jax.experimental import pallas as pl
from jax.experimental.pallas import tpu as pltpu
from jax.sharding import Mesh
from jax.sharding import PartitionSpec as P

MOST = 3
TOK = 16
CORES = 2
X, Y, ZH, ZL = 4, 8, 4, 4
Z = ZH * ZL
LANES = 128
BLOCK = 1024
BF16 = jnp.bfloat16
F32 = jnp.float32
MIB = 1024 * 1024


def pick_kernel(home, lane, *refs):
    blocks, tables, outs, pick = refs[:5], refs[5:10], refs[10:-1], refs[-1]
    slots, tokens = pick.shape

    @pl.when(pl.program_id(0) == 0)
    def _():
        at = lax.broadcasted_iota(jnp.int32, (slots, tokens), 1)
        line = jnp.where(at == home[...], 1.0, 0.0).astype(BF16)
        table = jnp.concatenate([ref[...] for ref in tables], axis=0)
        values = jnp.dot(line, table, preferred_element_type=F32)
        lanes = lax.broadcasted_iota(jnp.int32, values.shape, 1)
        value = jnp.sum(jnp.where(lanes == lane[...], values, 0.0), axis=1, keepdims=True)
        first = home[...] // TOK * TOK
        token = jnp.where(value > 0.0, value.astype(jnp.int32) - 1 + first, -1)
        pick[...] = jnp.where(at == token, 1.0, 0.0).astype(pick.dtype)

    held = jnp.concatenate([ref[...] for ref in blocks], axis=0)
    rows = jnp.dot(pick[...], held, preferred_element_type=F32).astype(BF16)
    share = rows.shape[0] // len(outs)
    for number, out in enumerate(outs):
        out[...] = rows[number * share : (number + 1) * share]


def pick_rows(home, lane, blocks, width):
    slots = home.shape[0]
    tokens = sum(block.shape[0] for block in blocks)
    last = width // LANES
    return pl.pallas_call(
        pick_kernel,
        grid=(width // BLOCK,),
        out_shape=[jax.ShapeDtypeStruct((slots // X, width), BF16)] * X,
        in_specs=[pl.BlockSpec((slots, 1), lambda i: (0, 0))] * 2
        + [pl.BlockSpec((block.shape[0], BLOCK), lambda i: (0, i)) for block in blocks]
        + [pl.BlockSpec((block.shape[0], LANES), lambda i: (0, last)) for block in blocks],
        out_specs=[pl.BlockSpec((slots // X, BLOCK), lambda i: (0, i))] * X,
        scratch_shapes=[pltpu.VMEM((slots, tokens), BF16)],
        compiler_params=pltpu.CompilerParams(vmem_limit_bytes=49 * MIB),
        cost_estimate=pl.CostEstimate(
            flops=2 * slots * tokens * width,
            bytes_accessed=2 * width * (slots + tokens),
            transcendentals=0,
        ),
        name="pick_rows",
    )(home, lane, *blocks, *blocks)


def joined(refs):
    return jnp.concatenate([ref[...] for ref in refs], axis=0)


def weight_kernel(left_own, left_pair, *refs):
    own, pair, out = refs[:X], refs[X : 2 * X], refs[2 * X]
    total = jnp.dot(left_own[...], joined(own), preferred_element_type=F32)
    total = total + jnp.dot(left_pair[...], joined(pair), preferred_element_type=F32)
    out[...] = total.astype(out.dtype)


def weight_term(left_own, left_pair, rows_own, rows_pair):
    half, slots = left_own.shape
    share, width = rows_own[0].shape
    return pl.pallas_call(
        weight_kernel,
        grid=(width // BLOCK,),
        out_shape=jax.ShapeDtypeStruct((half, width), BF16),
        in_specs=[pl.BlockSpec((half, slots), lambda i: (0, 0))] * 2
        + [pl.BlockSpec((share, BLOCK), lambda i: (0, i))] * (2 * X),
        out_specs=pl.BlockSpec((half, BLOCK), lambda i: (0, i)),
        compiler_params=pltpu.CompilerParams(vmem_limit_bytes=49 * MIB),
        cost_estimate=pl.CostEstimate(
            flops=4 * half * slots * width,
            bytes_accessed=2 * (2 * slots * width + half * width + 2 * half * slots),
            transcendentals=0,
        ),
        name="weight_term",
    )(left_own, left_pair, *rows_own, *rows_pair)


def hidden_kernel(weight, order, *refs):
    rows, (out, total) = refs[:X], refs[X:]
    step = pl.program_id(0)

    @pl.when(step == 0)
    def _():
        total[...] = jnp.zeros_like(total)

    total[...] += lax.dot_general(
        joined(rows), weight[...], (((1,), (1,)), ((), ())), preferred_element_type=F32
    )

    @pl.when(step == pl.num_programs(0) - 1)
    def _():
        rounded = total[...].astype(BF16)
        out[...] = jnp.dot(order[...], rounded, preferred_element_type=F32).astype(out.dtype)


def hidden_term(rows, weight, order):
    slots = order.shape[0]
    hidden, width = weight.shape[1:]
    return pl.pallas_call(
        hidden_kernel,
        grid=(width // BLOCK,),
        out_shape=jax.ShapeDtypeStruct((slots, hidden), BF16),
        in_specs=[
            pl.BlockSpec((None, hidden, BLOCK), lambda i: (0, 0, i)),
            pl.BlockSpec((slots, slots), lambda i: (0, 0)),
        ]
        + [pl.BlockSpec((slots // X, BLOCK), lambda i: (0, i))] * X,
        out_specs=pl.BlockSpec((slots, hidden), lambda i: (0, 0)),
        scratch_shapes=[pltpu.VMEM((slots, hidden), F32)],
        compiler_params=pltpu.CompilerParams(vmem_limit_bytes=49 * MIB),
        cost_estimate=pl.CostEstimate(
            flops=2 * slots * hidden * width,
            bytes_accessed=2 * (slots * width + hidden * width + slots * hidden),
            transcendentals=0,
        ),
        name="hidden_term",
    )(weight, order, *rows)


def shards(out_grad, hidden_acts, gate_weights, expert_idx, down_weight):
    tok_rows, top_count = expert_idx.shape
    routed = tok_rows * top_count
    width = out_grad.shape[1]
    hidden = hidden_acts.shape[2]
    half = hidden // CORES
    experts = X * Z
    slot_count = experts * MOST
    core = lax.axis_index("core")
    planes = ("zh", "zl")
    x_at = lax.axis_index("x")
    z_at = lax.axis_index(planes)
    swap = [(0, 1), (1, 0)]

    flat_expert = expert_idx.reshape(routed)
    member = (flat_expert[:, None] == jnp.arange(experts, dtype=jnp.int32)[None, :]).astype(BF16)
    row_line = jnp.arange(routed, dtype=jnp.int32)
    earlier_mask = (row_line[:, None] > row_line[None, :]).astype(BF16)
    earlier = jnp.dot(earlier_mask, member, preferred_element_type=F32)
    position = jnp.sum(earlier * member.astype(F32), axis=1).astype(jnp.int32)
    slot_index = flat_expert * MOST + position
    placement = (jnp.arange(slot_count, dtype=jnp.int32)[:, None] == slot_index[None, :]).astype(BF16)

    plane_of = (jnp.arange(Z, dtype=jnp.int32)[:, None] == (flat_expert % Z)[None, :]).astype(BF16)
    lane_of = (flat_expert // Z) * MOST + position
    token_of = (row_line // top_count + 1).astype(F32)
    token_at = jnp.where(
        lane_of[:, None] == jnp.arange(LANES, dtype=jnp.int32)[None, :], token_of[:, None], 0.0
    ).astype(BF16)
    table = jnp.dot(plane_of, token_at, preferred_element_type=F32).astype(BF16)

    own = lax.all_gather(jnp.concatenate([out_grad, table], axis=1), "zh", axis=0, tiled=True)

    def shifted(part, by):
        return lax.ppermute(part, planes, [(i, (i + by) % Z) for i in range(Z)])

    middle = own.shape[0] // 2
    blocks = (
        own,
        shifted(own, -1),
        shifted(own, 1),
        shifted(own[:middle], 2),
        shifted(own[middle:], -2),
    )

    gate_half = lax.optimization_barrier(gate_weights.astype(BF16)).astype(F32)
    flat_acts = hidden_acts.reshape(routed, hidden).astype(F32)
    gated = (gate_half.reshape(routed, 1) * flat_acts).astype(BF16)
    send_acts = jnp.dot(placement, gated, preferred_element_type=F32).astype(BF16)
    send_acts, _ = lax.optimization_barrier((send_acts, blocks[1:]))
    acts_in = lax.all_to_all(
        send_acts.reshape(experts, MOST, hidden),
        ("x",) + planes,
        split_axis=0,
        concat_axis=0,
        tiled=True,
    ).reshape(slot_count, hidden)

    slot = jnp.arange(slot_count, dtype=jnp.int32)
    per_x = Z * MOST
    held, high, rank = slot // (ZH * MOST) % ZL, slot // MOST % ZH, slot % MOST
    turn = jnp.where(held == 1, 1, jnp.where(held == 2, ZL - 1, jnp.where(held == 3, 2, 0)))
    source = high * ZL + (z_at + turn) % ZL
    steps = slot // per_x
    home_slot = (x_at + X - steps) % X * per_x + source * MOST + rank
    order = (slot[:, None] == home_slot[None, :]).astype(BF16)

    line = jnp.arange(hidden, dtype=jnp.int32)
    piece = hidden // (Y * CORES)
    unit = ((line % half) // piece * CORES + line // half) * piece + line % piece
    reorder = (unit[:, None] == line[None, :]).astype(BF16)
    acts_rows = lax.dot_general(
        order, acts_in, (((0,), (0,)), ((), ())), preferred_element_type=F32
    ).astype(BF16)
    left = lax.dot_general(
        reorder, acts_rows, (((1,), (1,)), ((), ())), preferred_element_type=F32
    ).astype(BF16)
    left_own = lax.dynamic_slice_in_dim(left, core * half, half, 0)
    left_away = lax.dynamic_slice_in_dim(left, (1 - core) * half, half, 0)

    home = (held * ZH + high) * tok_rows + z_at
    lane = (x_at + steps) % X * MOST + rank
    picked = pick_rows(home[:, None], lane[:, None], blocks, width)
    rows = [picked[0]] + [
        lax.ppermute(picked[by], "x", [(i, (i + by) % X) for i in range(X)]) for by in range(1, X)
    ]
    rows_pair = [lax.ppermute(part, "core", swap) for part in rows]
    left_pair = lax.ppermute(left_away, "core", swap)

    part = weight_term(left_own, left_pair, rows, rows_pair)
    summed = lax.psum_scatter(part, "y", scatter_dimension=0, tiled=True)

    grad_hidden = hidden_term(rows, down_weight, order)
    back = lax.all_to_all(
        grad_hidden.reshape(experts, MOST, hidden),
        ("x",) + planes,
        split_axis=0,
        concat_axis=0,
        tiled=True,
    ).reshape(slot_count, hidden)
    grad_tok = lax.dot_general(
        placement, back, (((0,), (0,)), ((), ())), preferred_element_type=F32
    )
    act_grad = (gate_half.reshape(routed, 1) * grad_tok).astype(BF16)
    score = jnp.sum(grad_tok * flat_acts, axis=1).astype(BF16).astype(F32)
    score = score.reshape(tok_rows, top_count)
    logit_grad = gate_weights * (score - jnp.sum(gate_weights * score, axis=1, keepdims=True))
    return act_grad.reshape(tok_rows, top_count, hidden), logit_grad, summed[None]


def solution(mesh):
    dims = Mesh(mesh.devices.reshape(Y, CORES, X, ZH, ZL), ("y", "core", "x", "zh", "zl"))
    experts = ("x", "zh", "zl")
    tokens = ("y", "core") + experts
    return jax.shard_map(
        shards,
        mesh=dims,
        in_specs=(
            P(tokens, None),
            P(tokens, None, None),
            P(tokens, None),
            P(tokens, None),
            P(experts, None, None),
        ),
        out_specs=(
            P(tokens, None, None),
            P(tokens, None),
            P(experts, ("y", "core"), None),
        ),
        check_vma=False,
    )
```

```python
import jax
import jax.numpy as jnp
import numpy as np
from jax import lax
from jax.experimental import pallas as pl
from jax.experimental.pallas import tpu as pltpu
from jax.sharding import Mesh
from jax.sharding import PartitionSpec as P

MOST = 3
TOK = 16
CORES = 2
X, Y, ZH, ZL = 4, 8, 4, 4
Z = ZH * ZL
LANES = 128
BLOCK = 1024
BF16 = jnp.bfloat16
F32 = jnp.float32
MIB = 1024 * 1024


def pick_kernel(home, lane, own, out):
    tokens, held = own.shape
    width = held - LANES
    rows = out.shape[0]
    at = lax.broadcasted_iota(jnp.int32, (home.shape[0], tokens), 1)
    line = jnp.where(at == home[...], 1.0, 0.0).astype(BF16)
    values = jnp.dot(line, own[:, width:], preferred_element_type=F32)
    lanes = lax.broadcasted_iota(jnp.int32, values.shape, 1)
    value = jnp.sum(jnp.where(lanes == lane[...], values, 0.0), axis=1, keepdims=True)
    first = home[...] // TOK * TOK
    token = jnp.where(value > 0.0, value.astype(jnp.int32) - 1 + first, -1)
    pick = jnp.where(at == token, 1.0, 0.0).astype(BF16)
    whole, lower, upper = pick[:rows], pick[rows : 2 * rows], pick[2 * rows :]
    for start in range(0, width, BLOCK):
        block = own[:, start : start + BLOCK]
        out[:, start : start + BLOCK] = jnp.dot(
            whole, block, preferred_element_type=F32
        ).astype(out.dtype)
    for start in range(0, width // 2, BLOCK):
        block = own[:, start : start + BLOCK]
        total = jnp.dot(lower, block, preferred_element_type=F32)
        block = own[:, width // 2 + start : width // 2 + start + BLOCK]
        total = total + jnp.dot(upper, block, preferred_element_type=F32)
        out[:, width + start : width + start + BLOCK] = total.astype(out.dtype)


def pick_rows(home, lane, own, rows):
    tokens, held = own.shape
    width = held - LANES
    return pl.pallas_call(
        pick_kernel,
        out_shape=jax.ShapeDtypeStruct((rows, width + width // 2), BF16),
        in_specs=[pl.BlockSpec(memory_space=pltpu.VMEM)] * 3,
        out_specs=pl.BlockSpec(memory_space=pltpu.VMEM),
        compiler_params=pltpu.CompilerParams(vmem_limit_bytes=32 * MIB),
        cost_estimate=pl.CostEstimate(
            flops=4 * rows * tokens * width,
            bytes_accessed=2 * width * (2 * rows + tokens),
            transcendentals=0,
        ),
        name="pick_rows",
    )(home, lane, own)


def joined(whole, halves):
    return jnp.concatenate([whole[...], halves[...]], axis=0)


def weight_kernel(own_a, own_b, pair_a, pair_b, rows_a, rows_b, other_a, other_b, out):
    left = jnp.concatenate([own_a[...], own_b[...]], axis=1)
    total = jnp.dot(left, joined(rows_a, rows_b), preferred_element_type=F32)
    left = jnp.concatenate([pair_a[...], pair_b[...]], axis=1)
    total = total + jnp.dot(left, joined(other_a, other_b), preferred_element_type=F32)
    out[...] = total.astype(out.dtype)


def weight_term(left_own, left_pair, rows_own, rows_pair):
    half = left_own.shape[0]
    rows, packed = rows_own.shape
    width = packed // 3 * 2
    blocks = width // BLOCK
    left_a = pl.BlockSpec((half, rows), lambda i: (0, 0))
    left_b = pl.BlockSpec((half, rows), lambda i: (0, 1 + i // (blocks // 2)))
    rows_a = pl.BlockSpec((rows, BLOCK), lambda i: (0, i))
    rows_b = pl.BlockSpec((rows, BLOCK), lambda i: (0, blocks + i % (blocks // 2)))
    return pl.pallas_call(
        weight_kernel,
        grid=(blocks,),
        out_shape=jax.ShapeDtypeStruct((half, width), BF16),
        in_specs=[left_a, left_b, left_a, left_b, rows_a, rows_b, rows_a, rows_b],
        out_specs=pl.BlockSpec((half, BLOCK), lambda i: (0, i)),
        compiler_params=pltpu.CompilerParams(vmem_limit_bytes=49 * MIB),
        cost_estimate=pl.CostEstimate(
            flops=8 * half * rows * width,
            bytes_accessed=2 * (2 * rows * packed + half * width),
            transcendentals=0,
        ),
        name="weight_term",
    )(left_own, left_own, left_pair, left_pair, rows_own, rows_own, rows_pair, rows_pair)


def hidden_kernel(rows_a, rows_b, weight, order, out, total):
    step = pl.program_id(0)
    rows = rows_a.shape[0]

    @pl.when(step == 0)
    def _():
        total[...] = jnp.zeros_like(total)

    now = lax.dot_general(
        joined(rows_a, rows_b),
        weight[...],
        (((1,), (1,)), ((), ())),
        preferred_element_type=F32,
    )
    total[:rows] += now[:rows]
    late = step >= pl.num_programs(0) // 2

    @pl.when(jnp.logical_not(late))
    def _():
        total[rows : 2 * rows] += now[rows:]

    @pl.when(late)
    def _():
        total[2 * rows :] += now[rows:]

    @pl.when(step == pl.num_programs(0) - 1)
    def _():
        rounded = total[...].astype(BF16)
        out[...] = jnp.dot(order[...], rounded, preferred_element_type=F32).astype(out.dtype)


def hidden_term(rows_own, weight, order):
    slots, spread = order.shape
    hidden, width = weight.shape[1:]
    rows = rows_own.shape[0]
    blocks = width // BLOCK
    return pl.pallas_call(
        hidden_kernel,
        grid=(blocks,),
        out_shape=jax.ShapeDtypeStruct((slots, hidden), BF16),
        in_specs=[
            pl.BlockSpec((rows, BLOCK), lambda i: (0, i)),
            pl.BlockSpec((rows, BLOCK), lambda i: (0, blocks + i % (blocks // 2))),
            pl.BlockSpec((None, hidden, BLOCK), lambda i: (0, 0, i)),
            pl.BlockSpec((slots, spread), lambda i: (0, 0)),
        ],
        out_specs=pl.BlockSpec((slots, hidden), lambda i: (0, 0)),
        scratch_shapes=[pltpu.VMEM((spread, hidden), F32)],
        compiler_params=pltpu.CompilerParams(vmem_limit_bytes=49 * MIB),
        cost_estimate=pl.CostEstimate(
            flops=4 * rows * hidden * width,
            bytes_accessed=2 * (2 * rows * width + hidden * width + slots * hidden),
            transcendentals=0,
        ),
        name="hidden_term",
    )(rows_own, rows_own, weight, order)


def shards(out_grad, hidden_acts, gate_weights, expert_idx, down_weight):
    tok_rows, top_count = expert_idx.shape
    routed = tok_rows * top_count
    width = out_grad.shape[1]
    hidden = hidden_acts.shape[2]
    half = hidden // CORES
    experts = X * Z
    slot_count = experts * MOST
    core = lax.axis_index("core")
    high_at = lax.axis_index("zh")
    swap = [(0, 1), (1, 0)]

    flat_expert = expert_idx.reshape(routed)
    member = (flat_expert[:, None] == jnp.arange(experts, dtype=jnp.int32)[None, :]).astype(BF16)
    row_line = jnp.arange(routed, dtype=jnp.int32)
    earlier_mask = (row_line[:, None] > row_line[None, :]).astype(BF16)
    earlier = jnp.dot(earlier_mask, member, preferred_element_type=F32)
    position = jnp.sum(earlier * member.astype(F32), axis=1).astype(jnp.int32)
    slot_index = flat_expert * MOST + position
    placement = (jnp.arange(slot_count, dtype=jnp.int32)[:, None] == slot_index[None, :]).astype(BF16)

    plane_of = (jnp.arange(Z, dtype=jnp.int32)[:, None] == (flat_expert % Z)[None, :]).astype(BF16)
    lane_of = (flat_expert // Z) * MOST + position
    token_of = (row_line // top_count + 1).astype(F32)
    token_at = jnp.where(
        lane_of[:, None] == jnp.arange(LANES, dtype=jnp.int32)[None, :], token_of[:, None], 0.0
    ).astype(BF16)
    table = jnp.dot(plane_of, token_at, preferred_element_type=F32).astype(BF16)

    own = lax.all_gather(jnp.concatenate([out_grad, table], axis=1), "zh", axis=0, tiled=True)

    gate_half = lax.optimization_barrier(gate_weights.astype(BF16)).astype(F32)
    flat_acts = hidden_acts.reshape(routed, hidden).astype(F32)
    gated = (gate_half.reshape(routed, 1) * flat_acts).astype(BF16)
    send_acts = jnp.dot(placement, gated, preferred_element_type=F32).astype(BF16)
    acts_in = lax.all_to_all(
        send_acts.reshape(experts, MOST, hidden),
        ("x", "zh", "zl"),
        split_axis=0,
        concat_axis=0,
        tiled=True,
    ).reshape(slot_count, hidden)

    packed = X * ZL * 8
    device, row = np.divmod(np.arange(packed, dtype=np.int32), 8)
    entry = np.concatenate([row, 8 + row % 4, 8 + row % 4])
    used = np.concatenate([row >= 0, row < 4, row >= 4])
    device = np.tile(device, 3)
    high, rank = np.divmod(entry, MOST)
    slot = device // ZL * (Z * MOST) + (high * ZL + device % ZL) * MOST + rank
    slot = np.where(used, slot, -1).astype(np.int32)
    order = (jnp.arange(slot_count, dtype=jnp.int32)[:, None] == slot[None, :]).astype(BF16)

    line = np.arange(hidden, dtype=np.int32)
    piece = hidden // (Y * CORES)
    unit = (((line % half) // piece * CORES + line // half) * piece + line % piece).astype(np.int32)
    reorder = (unit[:, None] == line[None, :]).astype(BF16)
    acts_rows = lax.dot_general(
        order, acts_in, (((0,), (0,)), ((), ())), preferred_element_type=F32
    ).astype(BF16)
    left = lax.dot_general(
        reorder, acts_rows, (((1,), (1,)), ((), ())), preferred_element_type=F32
    ).astype(BF16)
    left_own = lax.dynamic_slice_in_dim(left, core * half, half, 0)
    left_away = lax.dynamic_slice_in_dim(left, (1 - core) * half, half, 0)
    left_pair = lax.ppermute(left_away, "core", swap)

    home = np.where(used, high * tok_rows + device % ZL, -tok_rows).astype(np.int32)[:, None]
    lane = (device // ZL * MOST + rank).astype(np.int32)[:, None]
    picked = pick_rows(home + high_at * ZL, lane, own, packed)
    rows = lax.all_to_all(picked, ("x", "zl"), split_axis=0, concat_axis=0, tiled=True)
    rows, left_own, left_pair = lax.optimization_barrier((rows, left_own, left_pair))
    rows_pair = lax.ppermute(rows, "core", swap)

    part = weight_term(left_own, left_pair, rows, rows_pair)
    summed = lax.psum_scatter(part, "y", scatter_dimension=0, tiled=True)

    grad_hidden = hidden_term(rows, down_weight, order)
    back = lax.all_to_all(
        grad_hidden.reshape(experts, MOST, hidden),
        ("x", "zh", "zl"),
        split_axis=0,
        concat_axis=0,
        tiled=True,
    ).reshape(slot_count, hidden)
    grad_tok = lax.dot_general(
        placement, back, (((0,), (0,)), ((), ())), preferred_element_type=F32
    )
    act_grad = (gate_half.reshape(routed, 1) * grad_tok).astype(BF16)
    score = jnp.sum(grad_tok * flat_acts, axis=1).astype(BF16).astype(F32)
    score = score.reshape(tok_rows, top_count)
    logit_grad = gate_weights * (score - jnp.sum(gate_weights * score, axis=1, keepdims=True))
    return act_grad.reshape(tok_rows, top_count, hidden), logit_grad, summed[None]


def solution(mesh):
    dims = Mesh(mesh.devices.reshape(Y, CORES, X, ZH, ZL), ("y", "core", "x", "zh", "zl"))
    experts = ("x", "zh", "zl")
    tokens = ("y", "core") + experts
    return jax.shard_map(
        shards,
        mesh=dims,
        in_specs=(
            P(tokens, None),
            P(tokens, None, None),
            P(tokens, None),
            P(tokens, None),
            P(experts, None, None),
        ),
        out_specs=(
            P(tokens, None, None),
            P(tokens, None),
            P(experts, ("y", "core"), None),
        ),
        check_vma=False,
    )
```

```python
import jax
import jax.numpy as jnp
import numpy as np
from jax import lax
from jax.experimental import pallas as pl
from jax.experimental.pallas import tpu as pltpu
from jax.sharding import Mesh
from jax.sharding import PartitionSpec as P

MOST = 3
TOK = 16
CORES = 2
X, Y, ZH, ZL = 4, 8, 4, 4
Z = ZH * ZL
LANES = 128
BLOCK = 1024
BF16 = jnp.bfloat16
F32 = jnp.float32
MIB = 1024 * 1024


def pick_kernel(home, lane, source, own, acts, out):
    tokens, held = own.shape
    width = held - LANES
    rows = out.shape[0]
    at = lax.broadcasted_iota(jnp.int32, (home.shape[0], tokens), 1)
    line = jnp.where(at == home[...], 1.0, 0.0).astype(BF16)
    values = jnp.dot(line, own[:, width:], preferred_element_type=F32)
    lanes = lax.broadcasted_iota(jnp.int32, values.shape, 1)
    value = jnp.sum(jnp.where(lanes == lane[...], values, 0.0), axis=1, keepdims=True)
    first = home[...] // TOK * TOK
    token = jnp.where(value > 0.0, value.astype(jnp.int32) - 1 + first, -1)
    pick = jnp.where(at == token, 1.0, 0.0).astype(BF16)
    whole, lower, upper = pick[:rows], pick[rows : 2 * rows], pick[2 * rows :]
    for start in range(0, width, BLOCK):
        block = own[:, start : start + BLOCK]
        out[:, start : start + BLOCK] = jnp.dot(
            whole, block, preferred_element_type=F32
        ).astype(out.dtype)
    for start in range(0, width // 2, BLOCK):
        block = own[:, start : start + BLOCK]
        total = jnp.dot(lower, block, preferred_element_type=F32)
        block = own[:, width // 2 + start : width // 2 + start + BLOCK]
        total = total + jnp.dot(upper, block, preferred_element_type=F32)
        out[:, width + start : width + start + BLOCK] = total.astype(out.dtype)
    at = lax.broadcasted_iota(jnp.int32, (home.shape[0], acts.shape[0]), 1)
    pick = jnp.where(at == source[...], 1.0, 0.0).astype(BF16)
    whole, lower, upper = pick[:rows], pick[rows : 2 * rows], pick[2 * rows :]
    first = width + width // 2
    hidden = acts.shape[1]
    out[:, first : first + hidden] = jnp.dot(
        whole, acts[...], preferred_element_type=F32
    ).astype(out.dtype)
    total = jnp.dot(lower, acts[:, : hidden // 2], preferred_element_type=F32)
    total = total + jnp.dot(upper, acts[:, hidden // 2 :], preferred_element_type=F32)
    out[:, first + hidden :] = total.astype(out.dtype)


def pick_rows(home, lane, source, own, acts, rows):
    tokens, held = own.shape
    width = held - LANES
    packed = (width + acts.shape[1]) // 2 * 3
    return pl.pallas_call(
        pick_kernel,
        out_shape=jax.ShapeDtypeStruct((rows, packed), BF16),
        in_specs=[pl.BlockSpec(memory_space=pltpu.VMEM)] * 5,
        out_specs=pl.BlockSpec(memory_space=pltpu.VMEM),
        compiler_params=pltpu.CompilerParams(vmem_limit_bytes=32 * MIB),
        cost_estimate=pl.CostEstimate(
            flops=4 * rows * tokens * width,
            bytes_accessed=2 * width * (2 * rows + tokens),
            transcendentals=0,
        ),
        name="pick_rows",
    )(home, lane, source, own, acts)


def joined(whole, halves):
    return jnp.concatenate([whole[...], halves[...]], axis=0)


def weight_kernel(core, *refs):
    acts, rows, (out, left_own, left_pair) = refs[:4], refs[4:8], refs[8:]
    step = pl.program_id(0)
    slots, hidden = acts[0].shape
    half = hidden // 2

    @pl.when(step == 0)
    def _():
        line = lax.broadcasted_iota(jnp.int32, (slots, slots), 0)
        at = lax.broadcasted_iota(jnp.int32, (slots, slots), 1)
        lower = jnp.logical_and(line % 8 < 4, at == line + 4 * core[0])
        upper = jnp.logical_and(line % 8 >= 4, at == line - 4 + 4 * core[0])
        pick = jnp.concatenate([lower, upper], axis=0)
        pick = jnp.where(pick, 1.0, 0.0).astype(BF16)
        for whole, halves, left in ((acts[0], acts[1], left_own), (acts[2], acts[3], left_pair)):
            mine = jnp.where(core[0] == 0, whole[:, :half], whole[:, half:])
            spread = jnp.dot(pick, halves[...], preferred_element_type=F32)
            both = jnp.concatenate([mine.astype(F32), spread], axis=0)
            left[...] = jnp.transpose(both).astype(left.dtype)

    late = step >= pl.num_programs(0) // 2
    total = jnp.zeros(out.shape, F32)
    for whole, halves, left in ((rows[0], rows[1], left_own), (rows[2], rows[3], left_pair)):
        side = jnp.where(late, left[:, 2 * slots :], left[:, slots : 2 * slots])
        side = jnp.concatenate([left[:, :slots], side], axis=1)
        total = total + jnp.dot(side, joined(whole, halves), preferred_element_type=F32)
    out[...] = total.astype(out.dtype)


def weight_term(core, rows_own, rows_pair, width, hidden):
    rows, packed = rows_own.shape
    blocks = width // BLOCK
    half = hidden // 2
    first = width // 2 * 3
    acts_a = pl.BlockSpec((rows, hidden), lambda i: (0, first // hidden))
    acts_b = pl.BlockSpec((rows, half), lambda i: (0, (first + hidden) // half))
    rows_a = pl.BlockSpec((rows, BLOCK), lambda i: (0, i))
    rows_b = pl.BlockSpec((rows, BLOCK), lambda i: (0, blocks + i % (blocks // 2)))
    return pl.pallas_call(
        weight_kernel,
        grid=(blocks,),
        out_shape=jax.ShapeDtypeStruct((half, width), BF16),
        in_specs=[pl.BlockSpec(memory_space=pltpu.SMEM)]
        + [acts_a, acts_b, acts_a, acts_b, rows_a, rows_b, rows_a, rows_b],
        out_specs=pl.BlockSpec((half, BLOCK), lambda i: (0, i)),
        scratch_shapes=[pltpu.VMEM((half, 3 * rows), BF16)] * 2,
        compiler_params=pltpu.CompilerParams(vmem_limit_bytes=49 * MIB),
        cost_estimate=pl.CostEstimate(
            flops=8 * half * rows * width,
            bytes_accessed=2 * (2 * rows * packed + half * width),
            transcendentals=0,
        ),
        name="weight_term",
    )(core, *[rows_own] * 2, *[rows_pair] * 2, *[rows_own] * 2, *[rows_pair] * 2)


def hidden_kernel(rows_a, rows_b, weight, order, out, total):
    step = pl.program_id(0)
    rows = rows_a.shape[0]

    @pl.when(step == 0)
    def _():
        total[...] = jnp.zeros_like(total)

    now = lax.dot_general(
        joined(rows_a, rows_b),
        weight[...],
        (((1,), (1,)), ((), ())),
        preferred_element_type=F32,
    )
    total[:rows] += now[:rows]
    late = step >= pl.num_programs(0) // 2

    @pl.when(jnp.logical_not(late))
    def _():
        total[rows : 2 * rows] += now[rows:]

    @pl.when(late)
    def _():
        total[2 * rows :] += now[rows:]

    @pl.when(step == pl.num_programs(0) - 1)
    def _():
        rounded = total[...].astype(BF16)
        out[...] = jnp.dot(order[...], rounded, preferred_element_type=F32).astype(out.dtype)


def hidden_term(rows_own, weight, order):
    slots, spread = order.shape
    hidden, width = weight.shape[1:]
    rows = rows_own.shape[0]
    blocks = width // BLOCK
    return pl.pallas_call(
        hidden_kernel,
        grid=(blocks,),
        out_shape=jax.ShapeDtypeStruct((slots, hidden), BF16),
        in_specs=[
            pl.BlockSpec((rows, BLOCK), lambda i: (0, i)),
            pl.BlockSpec((rows, BLOCK), lambda i: (0, blocks + i % (blocks // 2))),
            pl.BlockSpec((None, hidden, BLOCK), lambda i: (0, 0, i)),
            pl.BlockSpec((slots, spread), lambda i: (0, 0)),
        ],
        out_specs=pl.BlockSpec((slots, hidden), lambda i: (0, 0)),
        scratch_shapes=[pltpu.VMEM((spread, hidden), F32)],
        compiler_params=pltpu.CompilerParams(vmem_limit_bytes=49 * MIB),
        cost_estimate=pl.CostEstimate(
            flops=4 * rows * hidden * width,
            bytes_accessed=2 * (2 * rows * width + hidden * width + slots * hidden),
            transcendentals=0,
        ),
        name="hidden_term",
    )(rows_own, rows_own, weight, order)


def shards(out_grad, hidden_acts, gate_weights, expert_idx, down_weight):
    tok_rows, top_count = expert_idx.shape
    routed = tok_rows * top_count
    width = out_grad.shape[1]
    hidden = hidden_acts.shape[2]
    experts = X * Z
    slot_count = experts * MOST
    high_at = lax.axis_index("zh")
    swap = [(0, 1), (1, 0)]

    flat_expert = expert_idx.reshape(routed)
    member = (flat_expert[:, None] == jnp.arange(experts, dtype=jnp.int32)[None, :]).astype(BF16)
    row_line = jnp.arange(routed, dtype=jnp.int32)
    earlier_mask = (row_line[:, None] > row_line[None, :]).astype(BF16)
    earlier = jnp.dot(earlier_mask, member, preferred_element_type=F32)
    position = jnp.sum(earlier * member.astype(F32), axis=1).astype(jnp.int32)
    slot_index = flat_expert * MOST + position
    placement = (jnp.arange(slot_count, dtype=jnp.int32)[:, None] == slot_index[None, :]).astype(BF16)

    plane_of = (jnp.arange(Z, dtype=jnp.int32)[:, None] == (flat_expert % Z)[None, :]).astype(BF16)
    lane_of = (flat_expert // Z) * MOST + position
    token_of = (row_line // top_count + 1).astype(F32)
    token_at = jnp.where(
        lane_of[:, None] == jnp.arange(LANES, dtype=jnp.int32)[None, :], token_of[:, None], 0.0
    ).astype(BF16)
    table = jnp.dot(plane_of, token_at, preferred_element_type=F32).astype(BF16)

    own = lax.all_gather(jnp.concatenate([out_grad, table], axis=1), "zh", axis=0, tiled=True)

    line = np.arange(hidden, dtype=np.int32)
    half = hidden // CORES
    piece = hidden // (Y * CORES)
    unit = (((line % half) // piece * CORES + line // half) * piece + line % piece).astype(np.int32)
    reorder = (unit[:, None] == line[None, :]).astype(BF16)
    gate_half = lax.optimization_barrier(gate_weights.astype(BF16)).astype(F32)
    flat_acts = hidden_acts.reshape(routed, hidden).astype(F32)
    gated = (gate_half.reshape(routed, 1) * flat_acts).astype(BF16)
    gated = lax.dot_general(
        gated, reorder, (((1,), (1,)), ((), ())), preferred_element_type=F32
    ).astype(BF16)
    group = flat_expert // Z * ZL + flat_expert % ZL
    out_index = (flat_expert // ZL % ZH * (X * ZL) + group) * MOST + position
    to_planes = (jnp.arange(slot_count, dtype=jnp.int32)[:, None] == out_index[None, :]).astype(BF16)
    send_acts = jnp.dot(to_planes, gated, preferred_element_type=F32).astype(BF16)
    acts = lax.all_to_all(send_acts, "zh", split_axis=0, concat_axis=0, tiled=True)

    packed = X * ZL * 8
    device, row = np.divmod(np.arange(packed, dtype=np.int32), 8)
    entry = np.concatenate([row, 8 + row % 4, 8 + row % 4])
    used = np.concatenate([row >= 0, row < 4, row >= 4])
    device = np.tile(device, 3)
    high, rank = np.divmod(entry, MOST)
    slot = device // ZL * (Z * MOST) + (high * ZL + device % ZL) * MOST + rank
    slot = np.where(used, slot, -1).astype(np.int32)
    order = (jnp.arange(slot_count, dtype=jnp.int32)[:, None] == slot[None, :]).astype(BF16)

    home = np.where(used, high * tok_rows + device % ZL, -tok_rows).astype(np.int32)[:, None]
    lane = (device // ZL * MOST + rank).astype(np.int32)[:, None]
    source = np.where(used, (high * (X * ZL) + device) * MOST + rank, -1).astype(np.int32)[:, None]
    picked = pick_rows(home + high_at * ZL, lane, source, own, acts, packed)
    rows = lax.all_to_all(picked, ("x", "zl"), split_axis=0, concat_axis=0, tiled=True)
    rows, order = lax.optimization_barrier((rows, order))
    rows_pair = lax.ppermute(rows, "core", [(0, 1), (1, 0)])

    core = lax.axis_index("core").astype(jnp.int32).reshape(1)
    part = weight_term(core, rows, rows_pair, out_grad.shape[1], hidden)
    summed = lax.psum_scatter(part, "y", scatter_dimension=0, tiled=True)

    grad_hidden = hidden_term(rows, down_weight, order)
    back = lax.all_to_all(
        grad_hidden.reshape(experts, MOST, hidden),
        ("x", "zh", "zl"),
        split_axis=0,
        concat_axis=0,
        tiled=True,
    ).reshape(slot_count, hidden)
    grad_tok = lax.dot_general(
        placement, back, (((0,), (0,)), ((), ())), preferred_element_type=F32
    )
    act_grad = (gate_half.reshape(routed, 1) * grad_tok).astype(BF16)
    score = jnp.sum(grad_tok * flat_acts, axis=1).astype(BF16).astype(F32)
    score = score.reshape(tok_rows, top_count)
    logit_grad = gate_weights * (score - jnp.sum(gate_weights * score, axis=1, keepdims=True))
    return act_grad.reshape(tok_rows, top_count, hidden), logit_grad, summed[None]


def solution(mesh):
    dims = Mesh(mesh.devices.reshape(Y, CORES, X, ZH, ZL), ("y", "core", "x", "zh", "zl"))
    experts = ("x", "zh", "zl")
    tokens = ("y", "core") + experts
    return jax.shard_map(
        shards,
        mesh=dims,
        in_specs=(
            P(tokens, None),
            P(tokens, None, None),
            P(tokens, None),
            P(tokens, None),
            P(experts, None, None),
        ),
        out_specs=(
            P(tokens, None, None),
            P(tokens, None),
            P(experts, ("y", "core"), None),
        ),
        check_vma=False,
    )
```

```python
import jax
import jax.numpy as jnp
import numpy as np
from jax import lax
from jax.experimental import pallas as pl
from jax.experimental.pallas import tpu as pltpu
from jax.sharding import Mesh
from jax.sharding import PartitionSpec as P

MOST = 3
TOK = 16
CORES = 2
X, Y, ZH, ZL = 4, 8, 4, 4
Z = ZH * ZL
LANES = 128
BLOCK = 1024
SHIFT = 2
BF16 = jnp.bfloat16
F32 = jnp.float32
MIB = 1024 * 1024


def pick_kernel(home, lane, own, out):
    tokens, held = own.shape
    width = held - LANES
    rows = out.shape[0]
    at = lax.broadcasted_iota(jnp.int32, (home.shape[0], tokens), 1)
    line = jnp.where(at == home[...], 1.0, 0.0).astype(BF16)
    values = jnp.dot(line, own[:, width:], preferred_element_type=F32)
    lanes = lax.broadcasted_iota(jnp.int32, values.shape, 1)
    value = jnp.sum(jnp.where(lanes == lane[...], values, 0.0), axis=1, keepdims=True)
    first = home[...] // TOK * TOK
    token = jnp.where(value > 0.0, value.astype(jnp.int32) - 1 + first, -1)
    pick = jnp.where(at == token, 1.0, 0.0).astype(BF16)
    whole, lower, upper = pick[:rows], pick[rows : 2 * rows], pick[2 * rows :]
    for start in range(0, width, BLOCK):
        block = own[:, start : start + BLOCK]
        out[:, start : start + BLOCK] = jnp.dot(
            whole, block, preferred_element_type=F32
        ).astype(out.dtype)
    for start in range(0, width // 2, BLOCK):
        block = own[:, start : start + BLOCK]
        total = jnp.dot(lower, block, preferred_element_type=F32)
        block = own[:, width // 2 + start : width // 2 + start + BLOCK]
        total = total + jnp.dot(upper, block, preferred_element_type=F32)
        out[:, width + start : width + start + BLOCK] = total.astype(out.dtype)


def pick_rows(home, lane, own, rows):
    tokens, held = own.shape
    width = held - LANES
    return pl.pallas_call(
        pick_kernel,
        out_shape=jax.ShapeDtypeStruct((rows, width + width // 2), BF16),
        in_specs=[pl.BlockSpec(memory_space=pltpu.VMEM)] * 3,
        out_specs=pl.BlockSpec(memory_space=pltpu.VMEM),
        compiler_params=pltpu.CompilerParams(vmem_limit_bytes=32 * MIB),
        cost_estimate=pl.CostEstimate(
            flops=4 * rows * tokens * width,
            bytes_accessed=2 * width * (2 * rows + tokens),
            transcendentals=0,
        ),
        name="pick_rows",
    )(home, lane, own)


def joined(whole, halves):
    return jnp.concatenate([whole[...], halves[...]], axis=0)


def weight_kernel(own_a, own_b, pair_a, pair_b, rows_a, rows_b, other_a, other_b, out):
    left = jnp.concatenate([own_a[...], own_b[...]], axis=1)
    total = jnp.dot(left, joined(rows_a, rows_b), preferred_element_type=F32)
    left = jnp.concatenate([pair_a[...], pair_b[...]], axis=1)
    total = total + jnp.dot(left, joined(other_a, other_b), preferred_element_type=F32)
    out[...] = total.astype(out.dtype)


def weight_term(left_own, left_pair, rows_own, rows_pair):
    half = left_own.shape[0]
    rows, packed = rows_own.shape
    width = packed // 3 * 2
    blocks = width // BLOCK
    left_a = pl.BlockSpec((half, rows), lambda i: (0, 0))
    left_b = pl.BlockSpec((half, rows), lambda i: (0, 1 + i // (blocks // 2)))
    rows_a = pl.BlockSpec((rows, BLOCK), lambda i: (0, i))
    rows_b = pl.BlockSpec((rows, BLOCK), lambda i: (0, blocks + i % (blocks // 2)))
    return pl.pallas_call(
        weight_kernel,
        grid=(blocks,),
        out_shape=jax.ShapeDtypeStruct((half, width), BF16),
        in_specs=[left_a, left_b, left_a, left_b, rows_a, rows_b, rows_a, rows_b],
        out_specs=pl.BlockSpec((half, BLOCK), lambda i: (0, i)),
        compiler_params=pltpu.CompilerParams(vmem_limit_bytes=49 * MIB),
        cost_estimate=pl.CostEstimate(
            flops=8 * half * rows * width,
            bytes_accessed=2 * (2 * rows * packed + half * width),
            transcendentals=0,
        ),
        name="weight_term",
    )(left_own, left_own, left_pair, left_pair, rows_own, rows_own, rows_pair, rows_pair)


def hidden_kernel(rows_a, rows_b, weight, order, out, total):
    step = pl.program_id(0)
    rows = rows_a.shape[0]

    @pl.when(step == 0)
    def _():
        total[...] = jnp.zeros_like(total)

    now = lax.dot_general(
        joined(rows_a, rows_b),
        weight[...],
        (((1,), (1,)), ((), ())),
        preferred_element_type=F32,
    )
    total[:rows] += now[:rows]
    late = step >= pl.num_programs(0) // 2

    @pl.when(jnp.logical_not(late))
    def _():
        total[rows : 2 * rows] += now[rows:]

    @pl.when(late)
    def _():
        total[2 * rows :] += now[rows:]

    @pl.when(step == pl.num_programs(0) - 1)
    def _():
        rounded = total[...].astype(BF16)
        out[...] = jnp.dot(order[...], rounded, preferred_element_type=F32).astype(out.dtype)


def hidden_term(rows_own, weight, order):
    slots, spread = order.shape
    hidden, width = weight.shape[1:]
    rows = rows_own.shape[0]
    blocks = width // BLOCK
    return pl.pallas_call(
        hidden_kernel,
        grid=(blocks,),
        out_shape=jax.ShapeDtypeStruct((slots, hidden), BF16),
        in_specs=[
            pl.BlockSpec((rows, BLOCK), lambda i: (0, i)),
            pl.BlockSpec((rows, BLOCK), lambda i: (0, blocks + i % (blocks // 2))),
            pl.BlockSpec((None, hidden, BLOCK), lambda i: (0, 0, i)),
            pl.BlockSpec((slots, spread), lambda i: (0, 0)),
        ],
        out_specs=pl.BlockSpec((slots, hidden), lambda i: (0, 0)),
        scratch_shapes=[pltpu.VMEM((spread, hidden), F32)],
        compiler_params=pltpu.CompilerParams(vmem_limit_bytes=49 * MIB),
        cost_estimate=pl.CostEstimate(
            flops=4 * rows * hidden * width,
            bytes_accessed=2 * (2 * rows * width + hidden * width + slots * hidden),
            transcendentals=0,
        ),
        name="hidden_term",
    )(rows_own, rows_own, weight, order)


def shards(out_grad, hidden_acts, gate_weights, expert_idx, down_weight):
    tok_rows, top_count = expert_idx.shape
    routed = tok_rows * top_count
    width = out_grad.shape[1]
    hidden = hidden_acts.shape[2]
    half = hidden // CORES
    experts = X * Z
    slot_count = experts * MOST
    core = lax.axis_index("core")
    z_at = lax.axis_index(("zh", "zl"))
    shift = core * SHIFT
    swap = [(0, 1), (1, 0)]

    flat_expert = expert_idx.reshape(routed)
    member = (flat_expert[:, None] == jnp.arange(experts, dtype=jnp.int32)[None, :]).astype(BF16)
    row_line = jnp.arange(routed, dtype=jnp.int32)
    earlier_mask = (row_line[:, None] > row_line[None, :]).astype(BF16)
    earlier = jnp.dot(earlier_mask, member, preferred_element_type=F32)
    position = jnp.sum(earlier * member.astype(F32), axis=1).astype(jnp.int32)
    slot_index = flat_expert * MOST + position
    placement = (jnp.arange(slot_count, dtype=jnp.int32)[:, None] == slot_index[None, :]).astype(BF16)

    plane_of = (jnp.arange(Z, dtype=jnp.int32)[:, None] == (flat_expert % Z)[None, :]).astype(BF16)
    lane_of = (flat_expert // Z) * MOST + position
    token_of = (row_line // top_count + 1).astype(F32)
    token_at = jnp.where(
        lane_of[:, None] == jnp.arange(LANES, dtype=jnp.int32)[None, :], token_of[:, None], 0.0
    ).astype(BF16)
    table = jnp.dot(plane_of, token_at, preferred_element_type=F32).astype(BF16)

    own = lax.all_gather(jnp.concatenate([out_grad, table], axis=1), "zh", axis=0, tiled=True)

    gate_half = lax.optimization_barrier(gate_weights.astype(BF16)).astype(F32)
    flat_acts = hidden_acts.reshape(routed, hidden).astype(F32)
    gated = (gate_half.reshape(routed, 1) * flat_acts).astype(BF16)
    send_acts = jnp.dot(placement, gated, preferred_element_type=F32).astype(BF16)
    acts_in = lax.all_to_all(
        send_acts.reshape(experts, MOST, hidden),
        ("x", "zh", "zl"),
        split_axis=0,
        concat_axis=0,
        tiled=True,
    ).reshape(slot_count, hidden)

    packed = X * ZL * 8
    device, row = np.divmod(np.arange(packed, dtype=np.int32), 8)
    entry = np.concatenate([row, 8 + row % 4, 8 + row % 4])
    used = np.concatenate([row >= 0, row < 4, row >= 4])
    device = np.tile(device, 3)
    high, rank = np.divmod(entry, MOST)
    across, along = np.divmod(device, ZL)
    slot = across * (Z * MOST) + (high * ZL + (along + shift) % ZL) * MOST + rank
    slot = jnp.where(used, slot, -1)
    order = (jnp.arange(slot_count, dtype=jnp.int32)[:, None] == slot[None, :]).astype(BF16)

    line = np.arange(hidden, dtype=np.int32)
    piece = hidden // (Y * CORES)
    unit = (((line % half) // piece * CORES + line // half) * piece + line % piece).astype(np.int32)
    reorder = (unit[:, None] == line[None, :]).astype(BF16)
    acts_rows = lax.dot_general(
        order, acts_in, (((0,), (0,)), ((), ())), preferred_element_type=F32
    ).astype(BF16)
    left = lax.dot_general(
        reorder, acts_rows, (((1,), (1,)), ((), ())), preferred_element_type=F32
    ).astype(BF16)
    left_own = lax.dynamic_slice_in_dim(left, core * half, half, 0)
    left_away = lax.dynamic_slice_in_dim(left, (1 - core) * half, half, 0)
    left_pair = lax.ppermute(left_away, "core", swap)

    start = (z_at + Z - shift) // ZL * ZL + shift
    plane = (start + along[:, None]) % Z
    home = jnp.where(used[:, None], (high * tok_rows)[:, None] + plane, -tok_rows)
    lane = (across * MOST + rank).astype(np.int32)[:, None]
    picked = pick_rows(home.astype(jnp.int32), lane, own, packed)
    lines = [
        [(c * X + x) * Z + (k * ZL + c * SHIFT + m) % Z for x in range(X) for m in range(ZL)]
        for c in range(CORES)
        for k in range(ZH)
    ]
    rows = lax.all_to_all(
        picked,
        ("core", "x", "zh", "zl"),
        split_axis=0,
        concat_axis=0,
        axis_index_groups=lines,
        tiled=True,
    )
    rows, left_own, left_pair = lax.optimization_barrier((rows, left_own, left_pair))
    rows_pair = lax.ppermute(rows, "core", swap)

    part = weight_term(left_own, left_pair, rows, rows_pair)
    summed = lax.psum_scatter(part, "y", scatter_dimension=0, tiled=True)

    grad_hidden = hidden_term(rows, down_weight, order)
    back = lax.all_to_all(
        grad_hidden.reshape(experts, MOST, hidden),
        ("x", "zh", "zl"),
        split_axis=0,
        concat_axis=0,
        tiled=True,
    ).reshape(slot_count, hidden)
    grad_tok = lax.dot_general(
        placement, back, (((0,), (0,)), ((), ())), preferred_element_type=F32
    )
    act_grad = (gate_half.reshape(routed, 1) * grad_tok).astype(BF16)
    score = jnp.sum(grad_tok * flat_acts, axis=1).astype(BF16).astype(F32)
    score = score.reshape(tok_rows, top_count)
    logit_grad = gate_weights * (score - jnp.sum(gate_weights * score, axis=1, keepdims=True))
    return act_grad.reshape(tok_rows, top_count, hidden), logit_grad, summed[None]


def solution(mesh):
    dims = Mesh(mesh.devices.reshape(Y, CORES, X, ZH, ZL), ("y", "core", "x", "zh", "zl"))
    experts = ("x", "zh", "zl")
    tokens = ("y", "core") + experts
    return jax.shard_map(
        shards,
        mesh=dims,
        in_specs=(
            P(tokens, None),
            P(tokens, None, None),
            P(tokens, None),
            P(tokens, None),
            P(experts, None, None),
        ),
        out_specs=(
            P(tokens, None, None),
            P(tokens, None),
            P(experts, ("y", "core"), None),
        ),
        check_vma=False,
    )
```

```python
import jax
import jax.numpy as jnp
import numpy as np
from jax import lax
from jax.experimental import pallas as pl
from jax.experimental.pallas import tpu as pltpu
from jax.sharding import Mesh
from jax.sharding import PartitionSpec as P

MOST = 3
TOK = 16
CORES = 2
X, Y, ZH, ZL = 4, 8, 4, 4
Z = ZH * ZL
LANES = 128
BLOCK = 1024
SHIFT = 2
BF16 = jnp.bfloat16
F32 = jnp.float32
MIB = 1024 * 1024


def pick_kernel(home, lane, own, out):
    tokens, held = own.shape
    width = held - LANES
    rows = out.shape[0]
    at = lax.broadcasted_iota(jnp.int32, (home.shape[0], tokens), 1)
    line = jnp.where(at == home[...], 1.0, 0.0).astype(BF16)
    values = jnp.dot(line, own[:, width:], preferred_element_type=F32)
    lanes = lax.broadcasted_iota(jnp.int32, values.shape, 1)
    value = jnp.sum(jnp.where(lanes == lane[...], values, 0.0), axis=1, keepdims=True)
    first = home[...] // TOK * TOK
    token = jnp.where(value > 0.0, value.astype(jnp.int32) - 1 + first, -1)
    pick = jnp.where(at == token, 1.0, 0.0).astype(BF16)
    whole, lower, upper = pick[:rows], pick[rows : 2 * rows], pick[2 * rows :]
    for start in range(0, width, BLOCK):
        block = own[:, start : start + BLOCK]
        out[:, start : start + BLOCK] = jnp.dot(
            whole, block, preferred_element_type=F32
        ).astype(out.dtype)
    for start in range(0, width // 2, BLOCK):
        block = own[:, start : start + BLOCK]
        total = jnp.dot(lower, block, preferred_element_type=F32)
        block = own[:, width // 2 + start : width // 2 + start + BLOCK]
        total = total + jnp.dot(upper, block, preferred_element_type=F32)
        out[:, width + start : width + start + BLOCK] = total.astype(out.dtype)


def pick_rows(home, lane, own, rows):
    tokens, held = own.shape
    width = held - LANES
    return pl.pallas_call(
        pick_kernel,
        out_shape=jax.ShapeDtypeStruct((rows, width + width // 2), BF16),
        in_specs=[pl.BlockSpec(memory_space=pltpu.VMEM)] * 3,
        out_specs=pl.BlockSpec(memory_space=pltpu.VMEM),
        compiler_params=pltpu.CompilerParams(vmem_limit_bytes=32 * MIB),
        cost_estimate=pl.CostEstimate(
            flops=4 * rows * tokens * width,
            bytes_accessed=2 * width * (2 * rows + tokens),
            transcendentals=0,
        ),
        name="pick_rows",
    )(home, lane, own)


def joined(whole, halves):
    return jnp.concatenate([whole[...], halves[...]], axis=0)


def weight_kernel(own_a, own_b, pair_a, pair_b, rows_a, rows_b, other_a, other_b, out):
    left = jnp.concatenate([own_a[...], own_b[...]], axis=1)
    total = jnp.dot(left, joined(rows_a, rows_b), preferred_element_type=F32)
    left = jnp.concatenate([pair_a[...], pair_b[...]], axis=1)
    total = total + jnp.dot(left, joined(other_a, other_b), preferred_element_type=F32)
    out[...] = total.astype(out.dtype)


def weight_term(left_own, left_pair, rows_own, rows_pair):
    half = left_own.shape[0]
    rows, packed = rows_own.shape
    width = packed // 3 * 2
    blocks = width // BLOCK
    left_a = pl.BlockSpec((half, rows), lambda i: (0, 0))
    left_b = pl.BlockSpec((half, rows), lambda i: (0, 1 + i // (blocks // 2)))
    rows_a = pl.BlockSpec((rows, BLOCK), lambda i: (0, i))
    rows_b = pl.BlockSpec((rows, BLOCK), lambda i: (0, blocks + i % (blocks // 2)))
    return pl.pallas_call(
        weight_kernel,
        grid=(blocks,),
        out_shape=jax.ShapeDtypeStruct((half, width), BF16),
        in_specs=[left_a, left_b, left_a, left_b, rows_a, rows_b, rows_a, rows_b],
        out_specs=pl.BlockSpec((half, BLOCK), lambda i: (0, i)),
        compiler_params=pltpu.CompilerParams(vmem_limit_bytes=49 * MIB),
        cost_estimate=pl.CostEstimate(
            flops=8 * half * rows * width,
            bytes_accessed=2 * (2 * rows * packed + half * width),
            transcendentals=0,
        ),
        name="weight_term",
    )(left_own, left_own, left_pair, left_pair, rows_own, rows_own, rows_pair, rows_pair)


def hidden_kernel(rows_a, rows_b, weight, order, out, total):
    step = pl.program_id(0)
    rows = rows_a.shape[0]

    @pl.when(step == 0)
    def _():
        total[...] = jnp.zeros_like(total)

    now = lax.dot_general(
        joined(rows_a, rows_b),
        weight[...],
        (((1,), (1,)), ((), ())),
        preferred_element_type=F32,
    )
    total[:rows] += now[:rows]
    late = step >= pl.num_programs(0) // 2

    @pl.when(jnp.logical_not(late))
    def _():
        total[rows : 2 * rows] += now[rows:]

    @pl.when(late)
    def _():
        total[2 * rows :] += now[rows:]

    @pl.when(step == pl.num_programs(0) - 1)
    def _():
        rounded = total[...].astype(BF16)
        out[...] = jnp.dot(order[...], rounded, preferred_element_type=F32).astype(out.dtype)


def hidden_term(rows_own, weight, order):
    slots, spread = order.shape
    hidden, width = weight.shape[1:]
    rows = rows_own.shape[0]
    blocks = width // BLOCK
    return pl.pallas_call(
        hidden_kernel,
        grid=(blocks,),
        out_shape=jax.ShapeDtypeStruct((slots, hidden), BF16),
        in_specs=[
            pl.BlockSpec((rows, BLOCK), lambda i: (0, i)),
            pl.BlockSpec((rows, BLOCK), lambda i: (0, blocks + i % (blocks // 2))),
            pl.BlockSpec((None, hidden, BLOCK), lambda i: (0, 0, i)),
            pl.BlockSpec((slots, spread), lambda i: (0, 0)),
        ],
        out_specs=pl.BlockSpec((slots, hidden), lambda i: (0, 0)),
        scratch_shapes=[pltpu.VMEM((spread, hidden), F32)],
        compiler_params=pltpu.CompilerParams(vmem_limit_bytes=49 * MIB),
        cost_estimate=pl.CostEstimate(
            flops=4 * rows * hidden * width,
            bytes_accessed=2 * (2 * rows * width + hidden * width + slots * hidden),
            transcendentals=0,
        ),
        name="hidden_term",
    )(rows_own, rows_own, weight, order)


def shards(out_grad, hidden_acts, gate_weights, expert_idx, down_weight):
    tok_rows, top_count = expert_idx.shape
    routed = tok_rows * top_count
    width = out_grad.shape[1]
    hidden = hidden_acts.shape[2]
    half = hidden // CORES
    experts = X * Z
    slot_count = experts * MOST
    core = lax.axis_index("core")
    z_at = lax.axis_index(("zh", "zl"))
    shift = core * SHIFT
    swap = [(0, 1), (1, 0)]

    flat_expert = expert_idx.reshape(routed)
    member = (flat_expert[:, None] == jnp.arange(experts, dtype=jnp.int32)[None, :]).astype(BF16)
    row_line = jnp.arange(routed, dtype=jnp.int32)
    earlier_mask = (row_line[:, None] > row_line[None, :]).astype(BF16)
    earlier = jnp.dot(earlier_mask, member, preferred_element_type=F32)
    position = jnp.sum(earlier * member.astype(F32), axis=1).astype(jnp.int32)
    slot_index = flat_expert * MOST + position
    placement = (jnp.arange(slot_count, dtype=jnp.int32)[:, None] == slot_index[None, :]).astype(BF16)

    plane_of = (jnp.arange(Z, dtype=jnp.int32)[:, None] == (flat_expert % Z)[None, :]).astype(BF16)
    lane_of = (flat_expert // Z) * MOST + position
    token_of = (row_line // top_count + 1).astype(F32)
    token_at = jnp.where(
        lane_of[:, None] == jnp.arange(LANES, dtype=jnp.int32)[None, :], token_of[:, None], 0.0
    ).astype(BF16)
    table = jnp.dot(plane_of, token_at, preferred_element_type=F32).astype(BF16)

    own = lax.all_gather(jnp.concatenate([out_grad, table], axis=1), "zh", axis=0, tiled=True)

    gate_half = lax.optimization_barrier(gate_weights.astype(BF16)).astype(F32)
    flat_acts = hidden_acts.reshape(routed, hidden).astype(F32)
    gated = (gate_half.reshape(routed, 1) * flat_acts).astype(BF16)
    send_acts = jnp.dot(placement, gated, preferred_element_type=F32).astype(BF16)
    send_acts, own = lax.optimization_barrier((send_acts, own))
    acts_in = lax.all_to_all(
        send_acts.reshape(experts, MOST, hidden),
        ("x", "zh", "zl"),
        split_axis=0,
        concat_axis=0,
        tiled=True,
    ).reshape(slot_count, hidden)

    packed = X * ZL * 8
    device, row = np.divmod(np.arange(packed, dtype=np.int32), 8)
    entry = np.concatenate([row, 8 + row % 4, 8 + row % 4])
    used = np.concatenate([row >= 0, row < 4, row >= 4])
    device = np.tile(device, 3)
    high, rank = np.divmod(entry, MOST)
    across, along = np.divmod(device, ZL)
    slot = across * (Z * MOST) + (high * ZL + (along + shift) % ZL) * MOST + rank
    slot = jnp.where(used, slot, -1)
    order = (jnp.arange(slot_count, dtype=jnp.int32)[:, None] == slot[None, :]).astype(BF16)

    line = np.arange(hidden, dtype=np.int32)
    piece = hidden // (Y * CORES)
    unit = (((line % half) // piece * CORES + line // half) * piece + line % piece).astype(np.int32)
    reorder = (unit[:, None] == line[None, :]).astype(BF16)
    acts_rows = lax.dot_general(
        order, acts_in, (((0,), (0,)), ((), ())), preferred_element_type=F32
    ).astype(BF16)
    left = lax.dot_general(
        reorder, acts_rows, (((1,), (1,)), ((), ())), preferred_element_type=F32
    ).astype(BF16)
    left_own = lax.dynamic_slice_in_dim(left, core * half, half, 0)
    left_away = lax.dynamic_slice_in_dim(left, (1 - core) * half, half, 0)
    left_pair = lax.ppermute(left_away, "core", swap)

    start = (z_at + Z - shift) // ZL * ZL + shift
    plane = (start + along[:, None]) % Z
    home = jnp.where(used[:, None], (high * tok_rows)[:, None] + plane, -tok_rows)
    lane = (across * MOST + rank).astype(np.int32)[:, None]
    picked = pick_rows(home.astype(jnp.int32), lane, own, packed)
    lines = [
        [(c * X + x) * Z + (k * ZL + c * SHIFT + m) % Z for x in range(X) for m in range(ZL)]
        for c in range(CORES)
        for k in range(ZH)
    ]
    rows = lax.all_to_all(
        picked,
        ("core", "x", "zh", "zl"),
        split_axis=0,
        concat_axis=0,
        axis_index_groups=lines,
        tiled=True,
    )
    rows, left_own, left_pair = lax.optimization_barrier((rows, left_own, left_pair))
    rows_pair = lax.ppermute(rows, "core", swap)

    part = weight_term(left_own, left_pair, rows, rows_pair)
    summed = lax.psum_scatter(part, "y", scatter_dimension=0, tiled=True)

    grad_hidden = hidden_term(rows, down_weight, order)
    back = lax.all_to_all(
        grad_hidden.reshape(experts, MOST, hidden),
        ("x", "zh", "zl"),
        split_axis=0,
        concat_axis=0,
        tiled=True,
    ).reshape(slot_count, hidden)
    grad_tok = lax.dot_general(
        placement, back, (((0,), (0,)), ((), ())), preferred_element_type=F32
    )
    act_grad = (gate_half.reshape(routed, 1) * grad_tok).astype(BF16)
    score = jnp.sum(grad_tok * flat_acts, axis=1).astype(BF16).astype(F32)
    score = score.reshape(tok_rows, top_count)
    logit_grad = gate_weights * (score - jnp.sum(gate_weights * score, axis=1, keepdims=True))
    return act_grad.reshape(tok_rows, top_count, hidden), logit_grad, summed[None]


def solution(mesh):
    dims = Mesh(mesh.devices.reshape(Y, CORES, X, ZH, ZL), ("y", "core", "x", "zh", "zl"))
    experts = ("x", "zh", "zl")
    tokens = ("y", "core") + experts
    return jax.shard_map(
        shards,
        mesh=dims,
        in_specs=(
            P(tokens, None),
            P(tokens, None, None),
            P(tokens, None),
            P(tokens, None),
            P(experts, None, None),
        ),
        out_specs=(
            P(tokens, None, None),
            P(tokens, None),
            P(experts, ("y", "core"), None),
        ),
        check_vma=False,
    )
```

```python
import jax
import jax.numpy as jnp
import numpy as np
from jax import lax
from jax.experimental import pallas as pl
from jax.experimental.pallas import tpu as pltpu
from jax.sharding import Mesh
from jax.sharding import PartitionSpec as P

MOST = 3
TOK = 16
CORES = 2
X, Y, ZH, ZL = 4, 8, 4, 4
Z = ZH * ZL
LANES = 128
BLOCK = 1024
SHIFT = 2
BF16 = jnp.bfloat16
F32 = jnp.float32
MIB = 1024 * 1024


def spread_kernel(slot, gate, acts, out):
    lines, packed = out.shape
    half = packed // MOST
    line = lax.broadcasted_iota(jnp.int32, (lines, acts.shape[0]), 0)
    for rank in range(MOST):
        weight = jnp.where(slot[...] == line // 2 * MOST + rank, gate[...], 0.0)
        lower = jnp.where(line % 2 == 0, weight, 0.0).astype(BF16)
        upper = jnp.where(line % 2 == 1, weight, 0.0).astype(BF16)
        total = jnp.dot(lower, acts[:, :half], preferred_element_type=F32)
        total = total + jnp.dot(upper, acts[:, half:], preferred_element_type=F32)
        out[:, rank * half : (rank + 1) * half] = total.astype(out.dtype)


def spread_acts(slot, gate, acts, lines):
    routed, hidden = acts.shape
    packed = hidden // 2 * MOST
    return pl.pallas_call(
        spread_kernel,
        out_shape=jax.ShapeDtypeStruct((lines, packed), BF16),
        in_specs=[pl.BlockSpec(memory_space=pltpu.VMEM)] * 3,
        out_specs=pl.BlockSpec(memory_space=pltpu.VMEM),
        compiler_params=pltpu.CompilerParams(vmem_limit_bytes=16 * MIB),
        cost_estimate=pl.CostEstimate(
            flops=4 * lines * routed * packed,
            bytes_accessed=2 * (routed * hidden + lines * packed),
            transcendentals=0,
        ),
        name="spread_acts",
    )(slot, gate, acts)


def pick_kernel(home, lane, own, out):
    tokens, held = own.shape
    width = held - LANES
    rows = out.shape[0]
    at = lax.broadcasted_iota(jnp.int32, (home.shape[0], tokens), 1)
    line = jnp.where(at == home[...], 1.0, 0.0).astype(BF16)
    values = jnp.dot(line, own[:, width:], preferred_element_type=F32)
    lanes = lax.broadcasted_iota(jnp.int32, values.shape, 1)
    value = jnp.sum(jnp.where(lanes == lane[...], values, 0.0), axis=1, keepdims=True)
    first = home[...] // TOK * TOK
    token = jnp.where(value > 0.0, value.astype(jnp.int32) - 1 + first, -1)
    pick = jnp.where(at == token, 1.0, 0.0).astype(BF16)
    whole, lower, upper = pick[:rows], pick[rows : 2 * rows], pick[2 * rows :]
    for start in range(0, width, BLOCK):
        block = own[:, start : start + BLOCK]
        out[:, start : start + BLOCK] = jnp.dot(
            whole, block, preferred_element_type=F32
        ).astype(out.dtype)
    for start in range(0, width // 2, BLOCK):
        block = own[:, start : start + BLOCK]
        total = jnp.dot(lower, block, preferred_element_type=F32)
        block = own[:, width // 2 + start : width // 2 + start + BLOCK]
        total = total + jnp.dot(upper, block, preferred_element_type=F32)
        out[:, width + start : width + start + BLOCK] = total.astype(out.dtype)


def pick_rows(home, lane, own, rows):
    tokens, held = own.shape
    width = held - LANES
    return pl.pallas_call(
        pick_kernel,
        out_shape=jax.ShapeDtypeStruct((rows, width + width // 2), BF16),
        in_specs=[pl.BlockSpec(memory_space=pltpu.VMEM)] * 3,
        out_specs=pl.BlockSpec(memory_space=pltpu.VMEM),
        compiler_params=pltpu.CompilerParams(vmem_limit_bytes=32 * MIB),
        cost_estimate=pl.CostEstimate(
            flops=4 * rows * tokens * width,
            bytes_accessed=2 * width * (2 * rows + tokens),
            transcendentals=0,
        ),
        name="pick_rows",
    )(home, lane, own)


def joined(whole, halves):
    return jnp.concatenate([whole[...], halves[...]], axis=0)


def weight_kernel(own_a, own_b, pair_a, pair_b, rows_a, rows_b, other_a, other_b, out):
    left = jnp.concatenate([own_a[...], own_b[...]], axis=1)
    total = jnp.dot(left, joined(rows_a, rows_b), preferred_element_type=F32)
    left = jnp.concatenate([pair_a[...], pair_b[...]], axis=1)
    total = total + jnp.dot(left, joined(other_a, other_b), preferred_element_type=F32)
    out[...] = total.astype(out.dtype)


def weight_term(left_own, left_pair, rows_own, rows_pair):
    half = left_own.shape[0]
    rows, packed = rows_own.shape
    width = packed // 3 * 2
    blocks = width // BLOCK
    left_a = pl.BlockSpec((half, rows), lambda i: (0, 0))
    left_b = pl.BlockSpec((half, rows), lambda i: (0, 1 + i // (blocks // 2)))
    rows_a = pl.BlockSpec((rows, BLOCK), lambda i: (0, i))
    rows_b = pl.BlockSpec((rows, BLOCK), lambda i: (0, blocks + i % (blocks // 2)))
    return pl.pallas_call(
        weight_kernel,
        grid=(blocks,),
        out_shape=jax.ShapeDtypeStruct((half, width), BF16),
        in_specs=[left_a, left_b, left_a, left_b, rows_a, rows_b, rows_a, rows_b],
        out_specs=pl.BlockSpec((half, BLOCK), lambda i: (0, i)),
        compiler_params=pltpu.CompilerParams(vmem_limit_bytes=49 * MIB),
        cost_estimate=pl.CostEstimate(
            flops=8 * half * rows * width,
            bytes_accessed=2 * (2 * rows * packed + half * width),
            transcendentals=0,
        ),
        name="weight_term",
    )(left_own, left_own, left_pair, left_pair, rows_own, rows_own, rows_pair, rows_pair)


def hidden_kernel(rows_a, rows_b, weight, order, out, total):
    step = pl.program_id(0)
    rows = rows_a.shape[0]

    @pl.when(step == 0)
    def _():
        total[...] = jnp.zeros_like(total)

    now = lax.dot_general(
        joined(rows_a, rows_b),
        weight[...],
        (((1,), (1,)), ((), ())),
        preferred_element_type=F32,
    )
    total[:rows] += now[:rows]
    late = step >= pl.num_programs(0) // 2

    @pl.when(jnp.logical_not(late))
    def _():
        total[rows : 2 * rows] += now[rows:]

    @pl.when(late)
    def _():
        total[2 * rows :] += now[rows:]

    @pl.when(step == pl.num_programs(0) - 1)
    def _():
        rounded = total[...].astype(BF16)
        out[...] = jnp.dot(order[...], rounded, preferred_element_type=F32).astype(out.dtype)


def hidden_term(rows_own, weight, order):
    slots, spread = order.shape
    hidden, width = weight.shape[1:]
    rows = rows_own.shape[0]
    blocks = width // BLOCK
    return pl.pallas_call(
        hidden_kernel,
        grid=(blocks,),
        out_shape=jax.ShapeDtypeStruct((slots, hidden), BF16),
        in_specs=[
            pl.BlockSpec((rows, BLOCK), lambda i: (0, i)),
            pl.BlockSpec((rows, BLOCK), lambda i: (0, blocks + i % (blocks // 2))),
            pl.BlockSpec((None, hidden, BLOCK), lambda i: (0, 0, i)),
            pl.BlockSpec((slots, spread), lambda i: (0, 0)),
        ],
        out_specs=pl.BlockSpec((slots, hidden), lambda i: (0, 0)),
        scratch_shapes=[pltpu.VMEM((spread, hidden), F32)],
        compiler_params=pltpu.CompilerParams(vmem_limit_bytes=49 * MIB),
        cost_estimate=pl.CostEstimate(
            flops=4 * rows * hidden * width,
            bytes_accessed=2 * (2 * rows * width + hidden * width + slots * hidden),
            transcendentals=0,
        ),
        name="hidden_term",
    )(rows_own, rows_own, weight, order)


def shards(out_grad, hidden_acts, gate_weights, expert_idx, down_weight):
    tok_rows, top_count = expert_idx.shape
    routed = tok_rows * top_count
    width = out_grad.shape[1]
    hidden = hidden_acts.shape[2]
    experts = X * Z
    slot_count = experts * MOST
    core = lax.axis_index("core")
    z_at = lax.axis_index(("zh", "zl"))
    shift = core * SHIFT
    swap = [(0, 1), (1, 0)]

    flat_expert = expert_idx.reshape(routed)
    member = (flat_expert[:, None] == jnp.arange(experts, dtype=jnp.int32)[None, :]).astype(BF16)
    row_line = jnp.arange(routed, dtype=jnp.int32)
    earlier_mask = (row_line[:, None] > row_line[None, :]).astype(BF16)
    earlier = jnp.dot(earlier_mask, member, preferred_element_type=F32)
    position = jnp.sum(earlier * member.astype(F32), axis=1).astype(jnp.int32)
    slot_index = flat_expert * MOST + position
    placement = (jnp.arange(slot_count, dtype=jnp.int32)[:, None] == slot_index[None, :]).astype(BF16)

    plane_of = (jnp.arange(Z, dtype=jnp.int32)[:, None] == (flat_expert % Z)[None, :]).astype(BF16)
    lane_of = (flat_expert // Z) * MOST + position
    token_of = (row_line // top_count + 1).astype(F32)
    token_at = jnp.where(
        lane_of[:, None] == jnp.arange(LANES, dtype=jnp.int32)[None, :], token_of[:, None], 0.0
    ).astype(BF16)
    table = jnp.dot(plane_of, token_at, preferred_element_type=F32).astype(BF16)

    own = lax.all_gather(jnp.concatenate([out_grad, table], axis=1), "zh", axis=0, tiled=True)

    gate_half = lax.optimization_barrier(gate_weights.astype(BF16)).astype(F32)
    flat_acts = hidden_acts.reshape(routed, hidden).astype(F32)
    half = hidden // CORES
    send_acts = spread_acts(
        slot_index.reshape(1, routed),
        gate_half.reshape(1, routed),
        hidden_acts.reshape(routed, hidden),
        2 * experts,
    )
    acts_in = lax.all_to_all(
        send_acts.reshape(experts, 2, MOST * half),
        ("x", "zh", "zl"),
        split_axis=0,
        concat_axis=0,
        tiled=True,
    )
    acts_in = jnp.transpose(acts_in.reshape(experts, 2, MOST, half), (0, 2, 1, 3))
    acts_in = acts_in.reshape(slot_count, hidden)

    packed = X * ZL * 8
    device, row = np.divmod(np.arange(packed, dtype=np.int32), 8)
    entry = np.concatenate([row, 8 + row % 4, 8 + row % 4])
    used = np.concatenate([row >= 0, row < 4, row >= 4])
    device = np.tile(device, 3)
    high, rank = np.divmod(entry, MOST)
    across, along = np.divmod(device, ZL)
    slot = across * (Z * MOST) + (high * ZL + (along + shift) % ZL) * MOST + rank
    slot = jnp.where(used, slot, -1)
    order = (jnp.arange(slot_count, dtype=jnp.int32)[:, None] == slot[None, :]).astype(BF16)

    line = np.arange(hidden, dtype=np.int32)
    piece = hidden // (Y * CORES)
    unit = (((line % half) // piece * CORES + line // half) * piece + line % piece).astype(np.int32)
    reorder = (unit[:, None] == line[None, :]).astype(BF16)
    acts_rows = lax.dot_general(
        order, acts_in, (((0,), (0,)), ((), ())), preferred_element_type=F32
    ).astype(BF16)
    left = lax.dot_general(
        reorder, acts_rows, (((1,), (1,)), ((), ())), preferred_element_type=F32
    ).astype(BF16)
    left_own = lax.dynamic_slice_in_dim(left, core * half, half, 0)
    left_away = lax.dynamic_slice_in_dim(left, (1 - core) * half, half, 0)
    left_pair = lax.ppermute(left_away, "core", swap)

    start = (z_at + Z - shift) // ZL * ZL + shift
    plane = (start + along[:, None]) % Z
    home = jnp.where(used[:, None], (high * tok_rows)[:, None] + plane, -tok_rows)
    lane = (across * MOST + rank).astype(np.int32)[:, None]
    picked = pick_rows(home.astype(jnp.int32), lane, own, packed)
    lines = [
        [(c * X + x) * Z + (k * ZL + c * SHIFT + m) % Z for x in range(X) for m in range(ZL)]
        for c in range(CORES)
        for k in range(ZH)
    ]
    rows = lax.all_to_all(
        picked,
        ("core", "x", "zh", "zl"),
        split_axis=0,
        concat_axis=0,
        axis_index_groups=lines,
        tiled=True,
    )
    rows, left_own, left_pair = lax.optimization_barrier((rows, left_own, left_pair))
    rows_pair = lax.ppermute(rows, "core", swap)

    part = weight_term(left_own, left_pair, rows, rows_pair)
    summed = lax.psum_scatter(part, "y", scatter_dimension=0, tiled=True)

    grad_hidden = hidden_term(rows, down_weight, order)
    back = lax.all_to_all(
        grad_hidden.reshape(experts, MOST, hidden),
        ("x", "zh", "zl"),
        split_axis=0,
        concat_axis=0,
        tiled=True,
    ).reshape(slot_count, hidden)
    grad_tok = lax.dot_general(
        placement, back, (((0,), (0,)), ((), ())), preferred_element_type=F32
    )
    act_grad = (gate_half.reshape(routed, 1) * grad_tok).astype(BF16)
    score = jnp.sum(grad_tok * flat_acts, axis=1).astype(BF16).astype(F32)
    score = score.reshape(tok_rows, top_count)
    logit_grad = gate_weights * (score - jnp.sum(gate_weights * score, axis=1, keepdims=True))
    return act_grad.reshape(tok_rows, top_count, hidden), logit_grad, summed[None]


def solution(mesh):
    dims = Mesh(mesh.devices.reshape(Y, CORES, X, ZH, ZL), ("y", "core", "x", "zh", "zl"))
    experts = ("x", "zh", "zl")
    tokens = ("y", "core") + experts
    return jax.shard_map(
        shards,
        mesh=dims,
        in_specs=(
            P(tokens, None),
            P(tokens, None, None),
            P(tokens, None),
            P(tokens, None),
            P(experts, None, None),
        ),
        out_specs=(
            P(tokens, None, None),
            P(tokens, None),
            P(experts, ("y", "core"), None),
        ),
        check_vma=False,
    )
```
